256 devices in a mesh: ctx: 32 (over z, y_lo, core), dec: 8 (over x, y_hi).
Axes of the slice: x: 4, y: 4 (y_hi: 2, y_lo: 2; y = y_hi * 2 + y_lo), z: 8, core: 2. Of those that a mesh axis runs over, the one named last changes fastest.
Arguments:
- hidden: bfloat16 [4096, 7168], P('ctx', 'dec'), may hold values from -6 to 6
- kv_weight: bfloat16 [7168, 576], P('dec'), may hold values from -0.0625 to 0.0625
- kv_gain: float32 [512], replicated, may hold values from 0.1 to 1.9
- queries: bfloat16 [4096, 64, 576], P('ctx', 'dec'), may hold values from -28 to 28
- group_order: int32 [64], replicated, may hold values from 0 to 63, as said below
- page_owner: int32 [32, 32], replicated, may hold values from 0 to 31, as said below
- page_slot: int32 [32, 32], replicated, may hold values from 0 to 31, as said below
Outputs:
- attended: bfloat16 [4096, 64, 512], P('ctx', 'dec')
- paged_cache: bfloat16 [1024, 2304], P('ctx')
The draws below stay inside these ranges and needn't reach their ends.
Inputs may be any that keep to these rules, and one draw needn't show every extreme that they name: `group_order`: each index of ctx holds two mirror blocks: some block b and the block b places from the end, in either order; every block appears once. `page_owner`: each row names every owner exactly 32 / 32 times. `page_slot`: the pages that reach one owner take its 32 slots once each.
All inputs are finite; a program needn't handle non-finite values.
Results may differ from the reference program's by a relative error of at most 0.012.
Values may be sent and summed in bfloat16 or wider, within the bound.
A program may use at most 128 MiB of HBM per device.

```python
import math
import jax
import jax.numpy as jnp
from jax import lax

D = 7168
LATENT = 512
KV_DIM = 576
HEADS = 64
TOKENS = 4096
HALF = 64
PAGE = 4
PAGES_DEV = 32
N_CTX = 32


def page_tables(key):
    owner_keys = jax.random.split(key, N_CTX)
    owners = jax.vmap(lambda one_key: jax.random.permutation(one_key, PAGES_DEV))(owner_keys) % N_CTX
    owners = owners.astype(jnp.int32)
    per_owner = PAGES_DEV // N_CTX
    onehot = (owners[:, :, None] == jnp.arange(N_CTX, dtype=jnp.int32)[None, None, :]).astype(jnp.int32)
    earlier = jnp.cumsum(onehot, axis=1) - onehot
    rank_here = jnp.sum(earlier * onehot, axis=2)
    incoming = jnp.arange(N_CTX, dtype=jnp.int32)[:, None] * per_owner + rank_here
    slot_keys = jax.random.split(jax.random.fold_in(key, 7), N_CTX)
    arrange = jax.vmap(lambda one_key: jax.random.permutation(one_key, PAGES_DEV))(slot_keys).astype(jnp.int32)
    slots = arrange[owners, incoming]
    return (owners, slots.astype(jnp.int32))


def draw_page_owner(key, part):
    return page_tables(key)[0]


def draw_page_slot(key, part):
    return page_tables(key)[1]


def draw_group_order(key, part):
    key = jax.random.fold_in(key, 5)
    holder_key, swap_key = jax.random.split(key)
    low_block = jax.random.permutation(holder_key, N_CTX).astype(jnp.int32)
    high_block = (2 * N_CTX - 1 - low_block).astype(jnp.int32)
    swapped = jax.random.randint(swap_key, (N_CTX,), 0, 2, dtype=jnp.int32)
    first = jnp.where(swapped == 1, high_block, low_block)
    second = jnp.where(swapped == 1, low_block, high_block)
    return jnp.stack([first, second], axis=1).reshape(-1).astype(jnp.int32)


def draw_queries(key, part):
    key = jax.random.fold_in(key, 3)
    base_key = jax.random.fold_in(key, 0)
    values = jnp.clip(jax.random.normal(base_key, (TOKENS, HEADS, KV_DIM), jnp.float32), -6.0, 6.0)
    return values.astype(jnp.bfloat16)


def shard_levels(stream_key, extent, shards, least, top_value):
    def one(dim, shards_of):
        heights = jax.random.uniform(jax.random.fold_in(jax.random.fold_in(stream_key, 6), dim), (shards_of,), jnp.float32, least / len(shards), top_value / len(shards))
        return jnp.repeat(jnp.exp(heights), extent[dim] // shards_of).reshape((-1,) + (1,) * (len(extent) - dim - 1))

    loudness = one(*shards[0])
    for cut in shards[1:]:
        loudness = loudness * one(*cut)
    return loudness


def scatter_about(stream_key, dims, deviation, reach, cuts=(), kind=jnp.bfloat16):
    entries = jax.random.normal(stream_key, dims, jnp.float32) * deviation
    if len(cuts) > 0:
        entries = shard_levels(stream_key, dims, cuts, -0.22, 0.18) * entries
    return jnp.clip(entries, min=-reach, max=reach).astype(kind)


def setup_inputs(seed: int = 0) -> dict:
    splits = jax.random.split(jax.random.key(seed), 8)
    hidden = scatter_about(splits[0], (TOKENS, D), 1.0, 6.0, ((0, 32), (1, 8)))
    kv_weight = scatter_about(splits[1], (D, KV_DIM), D ** -0.5, 0.0625, ((0, 8),))
    kv_gain = jnp.clip(1.0 + 0.18 * jax.random.normal(splits[2], (LATENT,), jnp.float32), 0.1, 1.9)
    queries = draw_queries(jax.random.fold_in(splits[7], 71), 0)
    group_order = draw_group_order(jax.random.fold_in(splits[7], 71), 0)
    page_owner = draw_page_owner(jax.random.fold_in(splits[7], 71), 0)
    page_slot = draw_page_slot(jax.random.fold_in(splits[7], 71), 0)
    return {"hidden": hidden, "kv_weight": kv_weight, "kv_gain": kv_gain, "queries": queries, "group_order": group_order, "page_owner": page_owner, "page_slot": page_slot}


SOFTMAX_SCALE = 192.0 ** (-0.5)
NORM_EPS = 1e-06

def finish_rows(projected, kv_gain, positions):
    width = kv_gain.shape[0]
    latent_part = projected[:, :width]
    scaled = latent_part * lax.rsqrt(lax.optimization_barrier(jnp.mean(latent_part * latent_part, axis=1, keepdims=True)) + NORM_EPS) * kv_gain
    rope_part = projected[:, width:]
    half_width = rope_part.shape[1] // 2
    frequency = 10000.0 ** (-(2.0 * jnp.arange(half_width, dtype=jnp.float32)) / rope_part.shape[1])
    angles = positions.astype(jnp.float32)[:, None] * frequency[None, :]
    first_half = rope_part[:, :half_width]
    second_half = rope_part[:, half_width:]
    cosine = jnp.cos(angles)
    sine = jnp.sin(angles)
    rotated = jnp.concatenate([first_half * cosine - second_half * sine, first_half * sine + second_half * cosine], axis=1)
    return jnp.concatenate([scaled, rotated], axis=1).astype(jnp.bfloat16)

def reference(hidden, kv_weight, kv_gain, queries, group_order, page_owner, page_slot):
    row_index = jnp.arange(TOKENS, dtype=jnp.int32)
    positions = (group_order[row_index // HALF] * HALF + row_index % HALF).astype(jnp.int32)
    projected = jnp.dot(hidden, kv_weight, preferred_element_type=jnp.float32)
    latent_cache = finish_rows(projected, kv_gain, positions)
    key_matrix = latent_cache.astype(jnp.float32)
    value_matrix = key_matrix[:, :LATENT]
    block_size = math.gcd(TOKENS, 256)

    def attend(block_id):
        first_row = (block_id * block_size).astype(jnp.int32)
        query_block = lax.dynamic_slice_in_dim(queries, first_row, block_size, 0).astype(jnp.float32)
        query_pos = lax.dynamic_slice_in_dim(positions, first_row, block_size, 0)
        scores = jnp.einsum('rhk,nk->rhn', query_block, key_matrix, precision=lax.Precision.HIGHEST) * SOFTMAX_SCALE
        allowed = positions[None, None, :] <= query_pos[:, None, None]
        highest = lax.optimization_barrier(jnp.max(jnp.where(allowed, scores, -jnp.inf), axis=-1, keepdims=True))
        weights = jnp.where(allowed, jnp.exp(scores - highest), 0.0)
        denominator = lax.optimization_barrier(jnp.sum(weights, axis=-1, keepdims=True))
        low_weights = weights.astype(jnp.bfloat16).astype(jnp.float32)
        mixed = jnp.einsum('rhn,nv->rhv', low_weights, value_matrix, precision=lax.Precision.HIGHEST)
        return (mixed / denominator).astype(jnp.bfloat16)
    attended = lax.map(attend, jnp.arange(TOKENS // block_size, dtype=jnp.int32)).reshape(TOKENS, HEADS, LATENT)
    destination = (page_owner * PAGES_DEV + page_slot).reshape(-1)
    page_rows = latent_cache.reshape(N_CTX * PAGES_DEV, PAGE * KV_DIM)
    paged_cache = jnp.zeros_like(page_rows).at[destination].set(page_rows)
    return (attended, paged_cache)
```

```python
import functools

import jax
import jax.numpy as jnp
import numpy as np
from jax import lax
from jax.experimental import pallas as pl
from jax.experimental.pallas import tpu as pltpu
from jax.sharding import PartitionSpec as P

MESH = pl.DeviceIdType.MESH
NX, NY, NZ = 4, 4, 8
HALF = 64
ROWS = 128
PIECE = 16
LAT = 512
ROT = 64
HEADS = 8
BLOCK = ROWS + PIECE
CHUNK = 4 * ROWS
PAGES = 32
EPS = 1e-6
LOG2E_SCALE = float(192.0 ** (-0.5) * np.log2(np.e))
NEG = -1e30
TILE_HEADS = 2


def device(x, y, z, core):
    return ((z * 2 + y % 2) * 2 + core, x * 2 + y // 2)


def remote(src, dst, send_sem, recv_sem, target):
    return pltpu.make_async_remote_copy(
        src_ref=src, dst_ref=dst, send_sem=send_sem, recv_sem=recv_sem, device_id=target, device_id_type=MESH
    )


def kernel(
    hidden_hbm, weight_hbm, gain_ref, freq_ref, queries_hbm, order_ref, owner_ref, slot_ref,
    out_ref, paged_ref,
    hid, wt, qt, part, sums, zbuf, gath, ql, qr, acc, top, den, bias, kpos, drow, page_lat, page_rot, krot,
    in_sem, rs_send, rs_recv, z_send, z_recv, b_send, b_recv, a_send, a_recv, s_send, s_recv,
):
    ctx = lax.axis_index("ctx")
    dec = lax.axis_index("dec")
    core = ctx % 2
    z = ctx // 4
    x = dec // 2
    y = (dec % 2) * 2 + (ctx // 2) % 2
    first = core == 0
    a = jnp.where(first, x, y)
    b = jnp.where(first, y, x)

    def at_ab(aa, bb):
        return device(jnp.where(first, aa, bb), jnp.where(first, bb, aa), z, core)

    rs_offsets = [(dx, dy) for dx in range(NX) for dy in range(2)][1:]

    def rs_device(dx, dy, sign):
        xx = (x + sign * dx + NX) % NX
        yh = (dec % 2 + dy) % 2
        return ctx, xx * 2 + yh

    barrier = pltpu.get_barrier_semaphore()
    partners = [rs_device(dx, dy, 1) for dx, dy in rs_offsets]
    partners += [device(x, y, (z + dz) % NZ, core) for dz in range(1, NZ)]
    partners += [at_ab(a, (b + d) % 4) for d in range(1, 4)]
    partners += [at_ab((a + d) % 4, b) for d in range(1, 4)]
    partners += [device(x, y, z, 1 - core)]
    for target in partners:
        pl.semaphore_signal(barrier, inc=1, device_id=target, device_id_type=MESH)

    loads = [
        pltpu.make_async_copy(hidden_hbm, hid, in_sem.at[0]),
        pltpu.make_async_copy(weight_hbm, wt, in_sem.at[1]),
        pltpu.make_async_copy(queries_hbm, qt, in_sem.at[2]),
    ]
    for load in loads:
        load.start()
    loads[0].wait()
    loads[1].wait()
    part[...] = lax.dot_general(
        hid[...], wt[...], (((1,), (1,)), ((), ())), preferred_element_type=jnp.float32
    ).reshape(part.shape)
    pl.semaphore_wait(barrier, len(partners))

    scatter = []
    for k, (dx, dy) in enumerate(rs_offsets):
        target = rs_device(dx, dy, 1)
        scatter.append(remote(part.at[target[1]], sums.at[k], rs_send.at[k], rs_recv.at[k], target))
        scatter[-1].start()

    start_pos = order_ref[ctx * 2 + dec // 4] * HALF + (dec % 4) * PIECE
    my_pos = (start_pos + lax.broadcasted_iota(jnp.int32, (PIECE, 128), 0)).astype(jnp.float32)
    angle = my_pos * freq_ref[...]
    cosine = jnp.cos(angle)
    sine = jnp.sin(angle)

    lane = lax.broadcasted_iota(jnp.int32, (1, ROWS), 1)
    lane_z = lane // PIECE
    lane_i = lane % PIECE
    mine = owner_ref[...] == ctx
    page_id = lax.broadcasted_iota(jnp.int32, (PAGES, PAGES), 1).astype(jnp.float32)
    page_of = jnp.sum(jnp.where(mine, page_id, 0.0), axis=1, keepdims=True)
    slot_of = jnp.sum(jnp.where(mine, slot_ref[...].astype(jnp.float32), 0.0), axis=1, keepdims=True)
    ctx_id = lax.broadcasted_iota(jnp.int32, (PAGES, ROWS), 0)
    ctx_lane = lax.broadcasted_iota(jnp.int32, (PAGES, ROWS), 1) // PIECE
    for cc in range(2):
        for ylo in range(2):
            picks = ctx_id == ctx_lane * 4 + (ylo * 2 + cc)
            page_z = jnp.sum(jnp.where(picks, page_of, 0.0), axis=0, keepdims=True).astype(jnp.int32)
            slot_z = jnp.sum(jnp.where(picks, slot_of, 0.0), axis=0, keepdims=True).astype(jnp.int32)
            for xhi in range(2):
                base = jnp.zeros((1, ROWS), jnp.int32)
                for zz in range(NZ):
                    base = jnp.where(lane_z == zz, order_ref[((zz * 2 + ylo) * 2 + cc) * 2 + xhi] * HALF, base)
                for xlo in range(2):
                    for yhi in range(2):
                        xx, yy = xhi * 2 + xlo, yhi * 2 + ylo
                        aa, bb = (xx, yy) if cc == 0 else (yy, xx)
                        row, cols = cc * 4 + aa, slice(bb * ROWS, (bb + 1) * ROWS)
                        kpos[row : row + 1, cols] = base + (xlo * 2 + yhi) * PIECE + lane_i
                        page = (xx * 2 + yhi) * 4 + lane_i // 4
                        drow[row : row + 1, cols] = jnp.where(page_z == page, (lane_i % 4) * PAGES + slot_z, -1)

    loads[2].wait()
    for h in range(HEADS):
        ql[h * ROWS : (h + 1) * ROWS, :] = qt[h, :LAT, :].T
        turned = qt[h, LAT:, :].T
        qr[h * ROWS : (h + 1) * ROWS, :] = jnp.concatenate([turned, turned], axis=1)
    acc[...] = jnp.zeros_like(acc)
    den[...] = jnp.zeros_like(den)
    top[...] = jnp.full_like(top, NEG)
    page_lat[...] = jnp.zeros_like(page_lat)
    page_rot[...] = jnp.zeros_like(page_rot)

    total = part[dec]
    for k, copy in enumerate(scatter):
        copy.wait_recv()
        total = total + sums[k]

    latent = total[:, :LAT]
    inverse = lax.rsqrt(jnp.mean(latent * latent, axis=1, keepdims=True) + EPS)
    latent = latent * inverse * gain_ref[...]
    half = ROT // 2
    r1, r2 = total[:, LAT : LAT + half], total[:, LAT + half :]
    c1, s1 = cosine[:, :half], sine[:, :half]
    turned = jnp.concatenate([r1 * c1 - r2 * s1, r1 * s1 + r2 * c1], axis=1)
    zbuf[z] = jnp.concatenate([latent, turned, turned], axis=1).astype(jnp.bfloat16)

    along_z = []
    for dz in range(1, NZ):
        copy = remote(zbuf.at[z], zbuf.at[z], z_send.at[dz], z_recv.at[dz], device(x, y, (z + dz) % NZ, core))
        copy.start()
        along_z.append(copy)
    for dz in range(1, NZ):
        came = (z - dz + NZ) % NZ
        remote(
            zbuf.at[came], zbuf.at[came], z_send.at[dz], z_recv.at[dz], device(x, y, (z + dz) % NZ, core)
        ).wait_recv()
    left = lax.broadcasted_iota(jnp.int32, (PIECE, 128), 1) < ROT
    mine_block = gath.at[core, a, b]
    for zz in range(NZ):
        mine_block[zz * PIECE : (zz + 1) * PIECE, :] = zbuf[zz, :, :LAT]
    for pair in range(NZ // 2):
        mine_block[ROWS:, pair * 128 : (pair + 1) * 128] = jnp.where(
            left, zbuf[2 * pair, :, LAT:], zbuf[2 * pair + 1, :, LAT:]
        )

    along_b = []
    for d in range(1, 4):
        copy = remote(mine_block, mine_block, b_send.at[d], b_recv.at[d], at_ab(a, (b + d) % 4))
        copy.start()
        along_b.append(copy)
    for d in range(1, 4):
        came = gath.at[core, a, (b - d + 4) % 4]
        remote(came, came, b_send.at[d], b_recv.at[d], at_ab(a, (b + d) % 4)).wait_recv()

    along_a = []
    strip = gath.at[core, a]
    for d in (1, 3, 2):
        copy = remote(strip, strip, a_send.at[d], a_recv.at[d], at_ab((a + d) % 4, b))
        copy.start()
        along_a.append(copy)

    token = lax.broadcasted_iota(jnp.int32, (ROWS, CHUNK), 0)
    q_pos = jnp.where(token < HALF, order_ref[ctx * 2], order_ref[ctx * 2 + 1]) * HALF + token % HALF
    page_row = lax.broadcasted_iota(jnp.int32, (ROWS, CHUNK), 0)
    tile_rows = TILE_HEADS * ROWS

    def attend(cc, aa):
        which = cc * 4 + aa
        bias[...] = jnp.where(kpos[pl.ds(which, 1), :] <= q_pos, 0.0, NEG)
        pick = jnp.where(drow[pl.ds(which, 1), :] == page_row, 1.0, 0.0).astype(jnp.bfloat16)
        for bb in range(4):
            for zz in range(NZ):
                rot = gath[cc, aa, bb, ROWS:, (zz // 2) * 128 : (zz // 2 + 1) * 128]
                keep = left if zz % 2 == 0 else jnp.logical_not(left)
                krot[bb * ROWS + zz * PIECE : bb * ROWS + (zz + 1) * PIECE, :] = jnp.where(
                    keep, rot, jnp.zeros_like(rot)
                )

        def keys():
            return jnp.concatenate([gath[cc, aa, bb, :ROWS, :] for bb in range(4)], axis=0)

        page_lat[...] += jnp.dot(pick, keys(), preferred_element_type=jnp.float32)
        page_rot[...] += jnp.dot(pick, krot[...], preferred_element_type=jnp.float32)

        @pl.loop(0, HEADS // TILE_HEADS)
        def _(tile):
            rows = pl.ds(pl.multiple_of(tile * tile_rows, tile_rows), tile_rows)
            nt = (((1,), (1,)), ((), ()))
            scores = lax.dot_general(ql[rows, :], keys(), nt, preferred_element_type=jnp.float32)
            scores += lax.dot_general(qr[rows, :], krot[...], nt, preferred_element_type=jnp.float32)
            scores += jnp.concatenate([bias[...]] * TILE_HEADS, axis=0)
            old = top[rows, :]
            new = jnp.maximum(old, jnp.max(scores, axis=1, keepdims=True))
            alpha = jnp.exp2((old - new) * LOG2E_SCALE)
            weights = jnp.exp2((scores - jnp.concatenate([new] * 4, axis=1)) * LOG2E_SCALE)
            top[rows, :] = new
            den[rows, :] = den[rows, :] * alpha + (
                (weights[:, :128] + weights[:, 128:256]) + (weights[:, 256:384] + weights[:, 384:])
            )
            mixed = jnp.dot(weights.astype(jnp.bfloat16), keys(), preferred_element_type=jnp.float32)
            acc[rows, :] = acc[rows, :] * jnp.concatenate([alpha] * 4, axis=1) + mixed

    sibling = device(x, y, z, 1 - core)

    @pl.loop(0, 4)
    def _(k):
        d = k ^ (k // 2)
        aa = (a - d + 4) % 4
        here = gath.at[core, aa]

        @pl.when(k > 0)
        def _():
            remote(here, here, a_send.at[d], a_recv.at[d], at_ab((a + d) % 4, b)).wait_recv()

        remote(here, here, s_send.at[d], s_recv.at[d], sibling).start()
        attend(core, aa)
        theirs = (b - d + 4) % 4
        there = gath.at[1 - core, theirs]
        remote(there, there, s_send.at[d], s_recv.at[d], sibling).wait_recv()
        attend(1 - core, theirs)

    @pl.loop(0, HEADS)
    def _(h):
        rows = pl.ds(pl.multiple_of(h * ROWS, ROWS), ROWS)
        whole = jnp.sum(den[rows, :], axis=1, keepdims=True)
        out_ref[h] = (acc[rows, :] / whole).astype(jnp.bfloat16)

    rotated = page_rot[:, :ROT] + page_rot[:, ROT:]
    width = LAT + ROT
    for j in range(4):
        rows = slice(j * PAGES, (j + 1) * PAGES)
        paged_ref[:, j * width : j * width + LAT] = page_lat[rows, :].astype(jnp.bfloat16)
        paged_ref[:, j * width + LAT : (j + 1) * width] = rotated[rows, :].astype(jnp.bfloat16)

    for copy in scatter + along_z + along_b + along_a:
        copy.wait_send()
    for d in range(4):
        here = gath.at[core, (a - d + 4) % 4]
        remote(here, here, s_send.at[d], s_recv.at[d], sibling).wait_send()


def body(hidden, kv_weight, kv_gain, queries, group_order, page_owner, page_slot):
    half = ROT // 2
    freq = 10000.0 ** (-(2.0 * np.arange(half, dtype=np.float32)) / ROT)
    freq = np.tile(freq.astype(np.float32), 4)[None, :]
    bf, f32 = jnp.bfloat16, jnp.float32
    vmem = pl.BlockSpec(memory_space=pltpu.VMEM)
    hbm = pl.BlockSpec(memory_space=pl.ANY)
    smem = pl.BlockSpec(memory_space=pltpu.SMEM)
    rows = HEADS * ROWS
    dma = pltpu.SemaphoreType.DMA
    attended, paged = pl.pallas_call(
        kernel,
        out_shape=(
            jax.ShapeDtypeStruct((HEADS, ROWS, LAT), bf),
            jax.ShapeDtypeStruct((PAGES, 4 * (LAT + ROT)), bf),
        ),
        in_specs=[hbm, hbm, vmem, vmem, hbm, smem, vmem, vmem],
        out_specs=(vmem, vmem),
        scratch_shapes=[
            pltpu.VMEM(hidden.shape, bf),
            pltpu.VMEM(kv_weight.shape[::-1], bf),
            pltpu.VMEM((HEADS, LAT + ROT, ROWS), bf),
            pltpu.VMEM((8, PIECE, LAT + ROT), f32),
            pltpu.VMEM((7, PIECE, LAT + ROT), f32),
            pltpu.VMEM((NZ, PIECE, LAT + 128), bf),
            pltpu.VMEM((2, 4, 4, BLOCK, LAT), bf),
            pltpu.VMEM((rows, LAT), bf),
            pltpu.VMEM((rows, 128), bf),
            pltpu.VMEM((rows, LAT), f32),
            pltpu.VMEM((rows, 128), f32),
            pltpu.VMEM((rows, 128), f32),
            pltpu.VMEM((ROWS, CHUNK), f32),
            pltpu.VMEM((8, CHUNK), jnp.int32),
            pltpu.VMEM((8, CHUNK), jnp.int32),
            pltpu.VMEM((ROWS, LAT), f32),
            pltpu.VMEM((ROWS, 128), f32),
            pltpu.VMEM((CHUNK, 128), bf),
            dma((3,)), dma((7,)), dma((7,)), dma((8,)), dma((8,)), dma((4,)), dma((4,)), dma((4,)), dma((4,)),
            dma((4,)), dma((4,)),
        ],
        name="cache_attention",
        compiler_params=pltpu.CompilerParams(
            collective_id=0, has_side_effects=True, vmem_limit_bytes=56 * 2**20
        ),
        cost_estimate=pl.CostEstimate(flops=9_000_000_000, bytes_accessed=4_000_000, transcendentals=4_000_000),
    )(
        hidden, kv_weight.T, kv_gain.reshape(1, -1), jnp.asarray(freq), queries.transpose(1, 2, 0),
        group_order, page_owner, page_slot,
    )
    return attended.transpose(1, 0, 2), paged


def solution(mesh):
    return jax.shard_map(
        body,
        mesh=mesh,
        in_specs=(P("ctx", "dec"), P("dec", None), P(), P("ctx", "dec", None), P(), P(), P()),
        out_specs=(P("ctx", "dec", None), P("ctx", None)),
        check_vma=False,
    )
```

```python
import functools

import jax
import jax.numpy as jnp
import numpy as np
from jax import lax
from jax.experimental import pallas as pl
from jax.experimental.pallas import tpu as pltpu
from jax.sharding import PartitionSpec as P

MESH = pl.DeviceIdType.MESH
NX, NY, NZ = 4, 4, 8
HALF = 64
ROWS = 128
PIECE = 16
LAT = 512
ROT = 64
HEADS = 8
BLOCK = ROWS + PIECE
CHUNK = 4 * ROWS
PAGES = 32
EPS = 1e-6
LOG2E_SCALE = float(192.0 ** (-0.5) * np.log2(np.e))
NEG = -1e30


def device(x, y, z, core):
    return ((z * 2 + y % 2) * 2 + core, x * 2 + y // 2)


def remote(src, dst, send_sem, recv_sem, target):
    return pltpu.make_async_remote_copy(
        src_ref=src, dst_ref=dst, send_sem=send_sem, recv_sem=recv_sem, device_id=target, device_id_type=MESH
    )


def kernel(
    hidden_hbm, weight_hbm, gain_ref, freq_ref, queries_hbm, order_ref, owner_ref, slot_ref,
    out_ref, paged_ref,
    hid, wt, qt, part, sums, zbuf, gath, q32, ql, qr, acc, top, den, qpos, kpos, drow, page_lat, page_rot, krot,
    in_sem, rs_send, rs_recv, z_send, z_recv, b_send, b_recv, a_send, a_recv, s_send, s_recv,
):
    ctx = lax.axis_index("ctx")
    dec = lax.axis_index("dec")
    core = ctx % 2
    z = ctx // 4
    x = dec // 2
    y = (dec % 2) * 2 + (ctx // 2) % 2
    first = core == 0
    a = jnp.where(first, x, y)
    b = jnp.where(first, y, x)

    def at_ab(aa, bb):
        return device(jnp.where(first, aa, bb), jnp.where(first, bb, aa), z, core)

    rs_offsets = [(dx, dy) for dx in range(NX) for dy in range(2)][1:]

    def rs_device(dx, dy, sign):
        xx = (x + sign * dx + NX) % NX
        yh = (dec % 2 + dy) % 2
        return ctx, xx * 2 + yh

    loads = [
        pltpu.make_async_copy(hidden_hbm, hid, in_sem.at[0]),
        pltpu.make_async_copy(weight_hbm, wt, in_sem.at[1]),
        pltpu.make_async_copy(queries_hbm, qt, in_sem.at[2]),
    ]
    for load in loads:
        load.start()

    barrier = pltpu.get_barrier_semaphore()
    partners = [rs_device(dx, dy, 1) for dx, dy in rs_offsets]
    partners += [device(x, y, (z + dz) % NZ, core) for dz in range(1, NZ)]
    partners += [at_ab(a, (b + d) % 4) for d in range(1, 4)]
    partners += [at_ab((a + d) % 4, b) for d in range(1, 4)]
    partners += [device(x, y, z, 1 - core)]
    for target in partners:
        pl.semaphore_signal(barrier, inc=1, device_id=target, device_id_type=MESH)

    loads[0].wait()
    loads[1].wait()
    part[...] = lax.dot_general(
        hid[...], wt[...], (((1,), (1,)), ((), ())), preferred_element_type=jnp.float32
    ).reshape(part.shape)
    pl.semaphore_wait(barrier, len(partners))

    scatter = []
    for k, (dx, dy) in enumerate(rs_offsets):
        target = rs_device(dx, dy, 1)
        scatter.append(remote(part.at[target[1]], sums.at[k], rs_send.at[k], rs_recv.at[k], target))
        scatter[-1].start()

    start_pos = order_ref[ctx * 2 + dec // 4] * HALF + (dec % 4) * PIECE
    my_pos = (start_pos + lax.broadcasted_iota(jnp.int32, (PIECE, 128), 0)).astype(jnp.float32)
    angle = my_pos * freq_ref[...]
    cosine = jnp.cos(angle)
    sine = jnp.sin(angle)

    lane = lax.broadcasted_iota(jnp.int32, (1, ROWS), 1)
    lane_z = lane // PIECE
    lane_i = lane % PIECE
    mine = owner_ref[...] == ctx
    page_id = lax.broadcasted_iota(jnp.int32, (PAGES, PAGES), 1).astype(jnp.float32)
    page_of = jnp.sum(jnp.where(mine, page_id, 0.0), axis=1, keepdims=True)
    slot_of = jnp.sum(jnp.where(mine, slot_ref[...].astype(jnp.float32), 0.0), axis=1, keepdims=True)
    ctx_id = lax.broadcasted_iota(jnp.int32, (PAGES, ROWS), 0)
    ctx_lane = lax.broadcasted_iota(jnp.int32, (PAGES, ROWS), 1) // PIECE
    for cc in range(2):
        for ylo in range(2):
            picks = ctx_id == ctx_lane * 4 + (ylo * 2 + cc)
            page_z = jnp.sum(jnp.where(picks, page_of, 0.0), axis=0, keepdims=True).astype(jnp.int32)
            slot_z = jnp.sum(jnp.where(picks, slot_of, 0.0), axis=0, keepdims=True).astype(jnp.int32)
            for xhi in range(2):
                base = jnp.zeros((1, ROWS), jnp.int32)
                for zz in range(NZ):
                    base = jnp.where(lane_z == zz, order_ref[((zz * 2 + ylo) * 2 + cc) * 2 + xhi] * HALF, base)
                for xlo in range(2):
                    for yhi in range(2):
                        xx, yy = xhi * 2 + xlo, yhi * 2 + ylo
                        aa, bb = (xx, yy) if cc == 0 else (yy, xx)
                        row, cols = cc * 4 + aa, slice(bb * ROWS, (bb + 1) * ROWS)
                        kpos[row : row + 1, cols] = base + (xlo * 2 + yhi) * PIECE + lane_i
                        page = (xx * 2 + yhi) * 4 + lane_i // 4
                        drow[row : row + 1, cols] = jnp.where(page_z == page, (lane_i % 4) * PAGES + slot_z, -1)

    loads[2].wait()
    for h in range(HEADS):
        turned = qt[h].T.astype(jnp.float32)
        turned = jnp.concatenate([turned, turned[:, LAT:]], axis=1)
        for g in range(5):
            q32[g, pl.ds(h, ROWS, stride=HEADS), :] = turned[:, g * 128 : (g + 1) * 128]
    for g in range(4):
        ql[:, g * 128 : (g + 1) * 128] = q32[g].astype(jnp.bfloat16)
    qr[...] = q32[4].astype(jnp.bfloat16)
    token = lax.broadcasted_iota(jnp.int32, qpos.shape, 0) // HEADS
    qpos[...] = jnp.where(token < HALF, order_ref[ctx * 2], order_ref[ctx * 2 + 1]) * HALF + token % HALF
    acc[...] = jnp.zeros_like(acc)
    den[...] = jnp.zeros_like(den)
    top[...] = jnp.full_like(top, NEG)
    page_lat[...] = jnp.zeros_like(page_lat)
    page_rot[...] = jnp.zeros_like(page_rot)

    total = part[dec]
    for k, copy in enumerate(scatter):
        copy.wait_recv()
        total = total + sums[k]

    latent = total[:, :LAT]
    inverse = lax.rsqrt(jnp.mean(latent * latent, axis=1, keepdims=True) + EPS)
    latent = latent * inverse * gain_ref[...]
    half = ROT // 2
    r1, r2 = total[:, LAT : LAT + half], total[:, LAT + half :]
    c1, s1 = cosine[:, :half], sine[:, :half]
    turned = jnp.concatenate([r1 * c1 - r2 * s1, r1 * s1 + r2 * c1], axis=1)
    zbuf[z] = jnp.concatenate([latent, turned, turned], axis=1).astype(jnp.bfloat16)

    along_z = []
    for dz in range(1, NZ):
        copy = remote(zbuf.at[z], zbuf.at[z], z_send.at[dz], z_recv.at[dz], device(x, y, (z + dz) % NZ, core))
        copy.start()
        along_z.append(copy)
    for dz in range(1, NZ):
        came = (z - dz + NZ) % NZ
        remote(
            zbuf.at[came], zbuf.at[came], z_send.at[dz], z_recv.at[dz], device(x, y, (z + dz) % NZ, core)
        ).wait_recv()
    left = lax.broadcasted_iota(jnp.int32, (PIECE, 128), 1) < ROT
    mine_block = gath.at[core, a, b]
    for zz in range(NZ):
        mine_block[zz * PIECE : (zz + 1) * PIECE, :] = zbuf[zz, :, :LAT]
    for pair in range(NZ // 2):
        mine_block[ROWS:, pair * 128 : (pair + 1) * 128] = jnp.where(
            left, zbuf[2 * pair, :, LAT:], zbuf[2 * pair + 1, :, LAT:]
        )

    sibling = device(x, y, z, 1 - core)

    def block(d, e):
        return gath.at[core, (a - d + 4) % 4, (b - e + 4) % 4]

    def along_b(e):
        return remote(mine_block, mine_block, b_send.at[e], b_recv.at[e], at_ab(a, (b + e) % 4))

    def along_a(d, e):
        return remote(block(0, e), block(0, e), a_send.at[d, e], a_recv.at[d, e], at_ab((a + d) % 4, b))

    def across(d, e):
        return remote(block(d, e), block(d, e), s_send.at[d, e], s_recv.at[d, e], sibling)

    for e in (1, 3, 2):
        along_b(e).start()
    for e in (0, 1, 3, 2):
        if e > 0:
            came = block(0, e)
            remote(came, came, b_send.at[e], b_recv.at[e], at_ab(a, (b + e) % 4)).wait_recv()
        for d in (1, 3, 2):
            along_a(d, e).start()
        across(0, e).start()

    page_row = lax.broadcasted_iota(jnp.int32, (ROWS, CHUNK), 0)

    def attend(cc, aa):
        which = cc * 4 + aa
        pick = jnp.where(drow[pl.ds(which, 1), :] == page_row, 1.0, 0.0).astype(jnp.bfloat16)
        for bb in range(4):
            for zz in range(NZ):
                rot = gath[cc, aa, bb, ROWS:, (zz // 2) * 128 : (zz // 2 + 1) * 128]
                keep = left if zz % 2 == 0 else jnp.logical_not(left)
                krot[bb * ROWS + zz * PIECE : bb * ROWS + (zz + 1) * PIECE, :] = jnp.where(
                    keep, rot, jnp.zeros_like(rot)
                )

        def keys():
            return jnp.concatenate([gath[cc, aa, bb, :ROWS, :] for bb in range(4)], axis=0)

        page_lat[...] += jnp.dot(pick, keys(), preferred_element_type=jnp.float32)
        page_rot[...] += jnp.dot(pick, krot[...], preferred_element_type=jnp.float32)

        nt = (((1,), (1,)), ((), ()))
        scores = lax.dot_general(ql[...], keys(), nt, preferred_element_type=jnp.float32)
        scores += lax.dot_general(qr[...], krot[...], nt, preferred_element_type=jnp.float32)
        limit = jnp.concatenate([qpos[...]] * 4, axis=1)
        scores = jnp.where(kpos[pl.ds(which, 1), :] <= limit, scores, NEG)
        old = top[...]
        new = jnp.maximum(old, jnp.max(scores, axis=1, keepdims=True))
        alpha = jnp.exp2((old - new) * LOG2E_SCALE)
        weights = jnp.exp2((scores - jnp.concatenate([new] * 4, axis=1)) * LOG2E_SCALE)
        top[...] = new
        den[...] = den[...] * alpha + (
            (weights[:, :128] + weights[:, 128:256]) + (weights[:, 256:384] + weights[:, 384:])
        )
        mixed = jnp.dot(weights.astype(jnp.bfloat16), keys(), preferred_element_type=jnp.float32)
        acc[...] = acc[...] * jnp.concatenate([alpha] * 4, axis=1) + mixed

    @pl.loop(0, 4)
    def _(k):
        d = k ^ (k // 2)

        @pl.when(k > 0)
        def _():
            for e in (0, 1, 3, 2):
                came = block(d, e)
                remote(came, came, a_send.at[d, e], a_recv.at[d, e], at_ab((a + d) % 4, b)).wait_recv()
                across(d, e).start()

        attend(core, (a - d + 4) % 4)
        theirs = (b - d + 4) % 4
        for e in (0, 1, 3, 2):
            there = gath.at[1 - core, theirs, (a - e + 4) % 4]
            remote(there, there, s_send.at[d, e], s_recv.at[d, e], sibling).wait_recv()
        attend(1 - core, theirs)

    out_ref[...] = (acc[...] / jnp.sum(den[...], axis=1, keepdims=True)).astype(jnp.bfloat16)

    rotated = page_rot[:, :ROT] + page_rot[:, ROT:]
    width = LAT + ROT
    for j in range(4):
        rows = slice(j * PAGES, (j + 1) * PAGES)
        paged_ref[:, j * width : j * width + LAT] = page_lat[rows, :].astype(jnp.bfloat16)
        paged_ref[:, j * width + LAT : (j + 1) * width] = rotated[rows, :].astype(jnp.bfloat16)

    for copy in scatter + along_z:
        copy.wait_send()
    for e in range(4):
        if e > 0:
            along_b(e).wait_send()
        for d in range(4):
            if d > 0:
                along_a(d, e).wait_send()
            across(d, e).wait_send()


def body(hidden, kv_weight, kv_gain, queries, group_order, page_owner, page_slot):
    half = ROT // 2
    freq = 10000.0 ** (-(2.0 * np.arange(half, dtype=np.float32)) / ROT)
    freq = np.tile(freq.astype(np.float32), 4)[None, :]
    bf, f32 = jnp.bfloat16, jnp.float32
    vmem = pl.BlockSpec(memory_space=pltpu.VMEM)
    hbm = pl.BlockSpec(memory_space=pl.ANY)
    smem = pl.BlockSpec(memory_space=pltpu.SMEM)
    rows = HEADS * ROWS
    dma = pltpu.SemaphoreType.DMA
    attended, paged = pl.pallas_call(
        kernel,
        out_shape=(
            jax.ShapeDtypeStruct((rows, LAT), bf),
            jax.ShapeDtypeStruct((PAGES, 4 * (LAT + ROT)), bf),
        ),
        in_specs=[hbm, hbm, vmem, vmem, hbm, smem, vmem, vmem],
        out_specs=(vmem, vmem),
        scratch_shapes=[
            pltpu.VMEM(hidden.shape, bf),
            pltpu.VMEM(kv_weight.shape[::-1], bf),
            pltpu.VMEM((HEADS, LAT + ROT, ROWS), bf),
            pltpu.VMEM((8, PIECE, LAT + ROT), f32),
            pltpu.VMEM((7, PIECE, LAT + ROT), f32),
            pltpu.VMEM((NZ, PIECE, LAT + 128), bf),
            pltpu.VMEM((2, 4, 4, BLOCK, LAT), bf),
            pltpu.VMEM((5, rows, 128), f32),
            pltpu.VMEM((rows, LAT), bf),
            pltpu.VMEM((rows, 128), bf),
            pltpu.VMEM((rows, LAT), f32),
            pltpu.VMEM((rows, 128), f32),
            pltpu.VMEM((rows, 128), f32),
            pltpu.VMEM((rows, 128), jnp.int32),
            pltpu.VMEM((8, CHUNK), jnp.int32),
            pltpu.VMEM((8, CHUNK), jnp.int32),
            pltpu.VMEM((ROWS, LAT), f32),
            pltpu.VMEM((ROWS, 128), f32),
            pltpu.VMEM((CHUNK, 128), bf),
            dma((3,)), dma((7,)), dma((7,)), dma((8,)), dma((8,)), dma((4,)), dma((4,)), dma((4, 4)), dma((4, 4)),
            dma((4, 4)), dma((4, 4)),
        ],
        name="cache_attention",
        compiler_params=pltpu.CompilerParams(
            collective_id=0, has_side_effects=True, vmem_limit_bytes=56 * 2**20
        ),
        cost_estimate=pl.CostEstimate(flops=9_000_000_000, bytes_accessed=4_000_000, transcendentals=4_000_000),
    )(
        hidden, kv_weight.T, kv_gain.reshape(1, -1), jnp.asarray(freq), queries.transpose(1, 2, 0),
        group_order, page_owner, page_slot,
    )
    return attended.reshape(ROWS, HEADS, LAT), paged


def solution(mesh):
    return jax.shard_map(
        body,
        mesh=mesh,
        in_specs=(P("ctx", "dec"), P("dec", None), P(), P("ctx", "dec", None), P(), P(), P()),
        out_specs=(P("ctx", "dec", None), P("ctx", None)),
        check_vma=False,
    )
```

```python
import functools

import jax
import jax.numpy as jnp
import numpy as np
from jax import lax
from jax.experimental import pallas as pl
from jax.experimental.pallas import tpu as pltpu
from jax.sharding import PartitionSpec as P

MESH = pl.DeviceIdType.MESH
NX, NY, NZ = 4, 4, 8
HALF = 64
ROWS = 128
PIECE = 16
LAT = 512
ROT = 64
HEADS = 8
BLOCK = ROWS + PIECE
CHUNK = 4 * ROWS
PAGES = 32
EPS = 1e-6
LOG2E_SCALE = float(192.0 ** (-0.5) * np.log2(np.e))
NEG = -1e30


def device(x, y, z, core):
    return ((z * 2 + y % 2) * 2 + core, x * 2 + y // 2)


def remote(src, dst, send_sem, recv_sem, target):
    return pltpu.make_async_remote_copy(
        src_ref=src, dst_ref=dst, send_sem=send_sem, recv_sem=recv_sem, device_id=target, device_id_type=MESH
    )


def kernel(
    hidden_hbm, weight_hbm, gain_ref, freq_ref, queries_hbm, order_ref, owner_ref, slot_ref,
    out_hbm, paged_ref,
    hid, wt, qt, part, sums, zbuf, gath, q32, ql, qr, acc, top, den, qpos, kpos, drow, page_lat, page_rot, krot, done,
    in_sem, rs_send, rs_recv, z_send, z_recv, b_send, b_recv, a_send, a_recv, s_send, s_recv, out_sem,
):
    ctx = lax.axis_index("ctx")
    dec = lax.axis_index("dec")
    core = ctx % 2
    z = ctx // 4
    x = dec // 2
    y = (dec % 2) * 2 + (ctx // 2) % 2
    first = core == 0
    a = jnp.where(first, x, y)
    b = jnp.where(first, y, x)

    def at_ab(aa, bb):
        return device(jnp.where(first, aa, bb), jnp.where(first, bb, aa), z, core)

    half_me = (x // 2 + dec % 2) % 2
    sub_me = (x % 2) * 2 + dec % 2
    low_at = jnp.minimum(order_ref[ctx * 2], order_ref[ctx * 2 + 1]) * HALF
    high_at = jnp.maximum(order_ref[ctx * 2], order_ref[ctx * 2 + 1]) * HALF
    turn = jnp.full((HALF * HEADS, LAT), order_ref[ctx * 2], jnp.int32) > order_ref[ctx * 2 + 1]

    rs_offsets = [(dx, dy) for dx in range(NX) for dy in range(2)][1:]

    def rs_device(dx, dy, sign):
        xx = (x + sign * dx + NX) % NX
        yh = (dec % 2 + dy) % 2
        return ctx, xx * 2 + yh

    loads = [pltpu.make_async_copy(hidden_hbm, hid, in_sem.at[0])]
    for k in range(4):
        span = pl.ds(k * 144, 144)
        loads.append(pltpu.make_async_copy(weight_hbm.at[span], wt.at[span], in_sem.at[1 + k]))
    for k in range(4):
        span = pl.ds(k * 2, 2)
        loads.append(pltpu.make_async_copy(queries_hbm.at[span], qt.at[span], in_sem.at[5 + k]))
    for load in loads:
        load.start()

    barrier = pltpu.get_barrier_semaphore()
    partners = [rs_device(dx, dy, 1) for dx, dy in rs_offsets]
    partners += [device(x, y, (z + dz) % NZ, core) for dz in range(1, NZ)]
    partners += [at_ab(a, (b + d) % 4) for d in range(1, 4)]
    partners += [at_ab((a + d) % 4, b) for d in range(1, 4)]
    partners += [device(x, y, z, 1 - core)]
    for target in partners:
        pl.semaphore_signal(barrier, inc=1, device_id=target, device_id_type=MESH)

    for load in loads[:5]:
        load.wait()
    projected = lax.dot_general(
        hid[...], wt[...], (((1,), (1,)), ((), ())), preferred_element_type=jnp.float32
    )
    upper, lower = projected[:HALF], projected[HALF:]
    swap = jnp.full(upper.shape, order_ref[ctx * 2], jnp.int32) > order_ref[ctx * 2 + 1]
    part[:4] = jnp.where(swap, lower, upper).reshape(4, PIECE, LAT + ROT)
    part[4:] = jnp.where(swap, upper, lower).reshape(4, PIECE, LAT + ROT)
    pl.semaphore_wait(barrier, len(partners))

    scatter = []
    for k, (dx, dy) in enumerate(rs_offsets):
        target = rs_device(dx, dy, 1)
        tx, ty = target[1] // 2, target[1] % 2
        theirs = ((tx // 2 + ty) % 2) * 4 + (tx % 2) * 2 + ty
        scatter.append(remote(part.at[theirs], sums.at[k], rs_send.at[k], rs_recv.at[k], target))
        scatter[-1].start()

    start_pos = jnp.where(half_me == 0, low_at, high_at) + sub_me * PIECE
    my_pos = (start_pos + lax.broadcasted_iota(jnp.int32, (PIECE, 128), 0)).astype(jnp.float32)
    angle = my_pos * freq_ref[...]
    cosine = jnp.cos(angle)
    sine = jnp.sin(angle)

    lane = lax.broadcasted_iota(jnp.int32, (1, ROWS), 1)
    lane_z = lane // PIECE
    lane_i = lane % PIECE
    mine = owner_ref[...] == ctx
    page_id = lax.broadcasted_iota(jnp.int32, (PAGES, PAGES), 1).astype(jnp.float32)
    page_of = jnp.sum(jnp.where(mine, page_id, 0.0), axis=1, keepdims=True)
    slot_of = jnp.sum(jnp.where(mine, slot_ref[...].astype(jnp.float32), 0.0), axis=1, keepdims=True)
    ctx_id = lax.broadcasted_iota(jnp.int32, (PAGES, ROWS), 0)
    ctx_lane = lax.broadcasted_iota(jnp.int32, (PAGES, ROWS), 1) // PIECE
    for cc in range(2):
        for ylo in range(2):
            picks = ctx_id == ctx_lane * 4 + (ylo * 2 + cc)
            page_z = jnp.sum(jnp.where(picks, page_of, 0.0), axis=0, keepdims=True).astype(jnp.int32)
            slot_z = jnp.sum(jnp.where(picks, slot_of, 0.0), axis=0, keepdims=True).astype(jnp.int32)
            bases = [jnp.zeros((1, ROWS), jnp.int32)] * 2
            turned = jnp.zeros((1, ROWS), jnp.int32)
            for zz in range(NZ):
                at = ((zz * 2 + ylo) * 2 + cc) * 2
                one, two = order_ref[at], order_ref[at + 1]
                bases[0] = jnp.where(lane_z == zz, jnp.minimum(one, two) * HALF, bases[0])
                bases[1] = jnp.where(lane_z == zz, jnp.maximum(one, two) * HALF, bases[1])
                turned = jnp.where(lane_z == zz, jnp.where(one > two, PAGES // 2, 0), turned)
            page_z = jnp.bitwise_xor(page_z, turned)
            for xx in range(4):
                for yhi in range(2):
                    aa, bb = (xx, yhi * 2 + ylo) if cc == 0 else (yhi * 2 + ylo, xx)
                    half, sub = (xx // 2 + yhi) % 2, (xx % 2) * 2 + yhi
                    at = (half * 2 + bb % 2) * ROWS
                    row, cols = cc * 4 + aa, slice(at, at + ROWS)
                    kpos[row : row + 1, cols] = bases[half] + sub * PIECE + lane_i
                    page = half * (PAGES // 2) + sub * 4 + lane_i // 4
                    drow[row : row + 1, cols] = jnp.where(page_z == page, (lane_i % 4) * PAGES + slot_z, -1)

    for load in loads[5:]:
        load.wait()
    rows = HEADS * ROWS
    for h in range(HEADS):
        turned = qt[h].T.astype(jnp.float32)
        turned = jnp.concatenate([turned, turned[:, LAT:]], axis=1)
        for g in range(5):
            q32[g, pl.ds(h, ROWS, stride=HEADS), :] = turned[:, g * 128 : (g + 1) * 128]
    for g in range(5):
        upper, lower = q32[g, : rows // 2, :], q32[g, rows // 2 :, :]
        swap = turn[:, :128]
        ordered = jnp.concatenate([jnp.where(swap, lower, upper), jnp.where(swap, upper, lower)], axis=0)
        if g < 4:
            ql[:, g * 128 : (g + 1) * 128] = ordered.astype(jnp.bfloat16)
        else:
            qr[...] = ordered.astype(jnp.bfloat16)
    qpos[...] = lax.broadcasted_iota(jnp.int32, qpos.shape, 0) // HEADS
    acc[...] = jnp.zeros_like(acc)
    den[...] = jnp.zeros_like(den)
    top[...] = jnp.full_like(top, NEG)
    page_lat[...] = jnp.zeros_like(page_lat)
    page_rot[...] = jnp.zeros_like(page_rot)

    total = part[half_me * 4 + sub_me]
    for k, copy in enumerate(scatter):
        copy.wait_recv()
        total = total + sums[k]

    latent = total[:, :LAT]
    inverse = lax.rsqrt(jnp.mean(latent * latent, axis=1, keepdims=True) + EPS)
    latent = latent * inverse * gain_ref[...]
    half = ROT // 2
    r1, r2 = total[:, LAT : LAT + half], total[:, LAT + half :]
    c1, s1 = cosine[:, :half], sine[:, :half]
    turned = jnp.concatenate([r1 * c1 - r2 * s1, r1 * s1 + r2 * c1], axis=1)
    zbuf[z] = jnp.concatenate([latent, turned, turned], axis=1).astype(jnp.bfloat16)

    along_z = []
    for dz in range(1, NZ):
        copy = remote(zbuf.at[z], zbuf.at[z], z_send.at[dz], z_recv.at[dz], device(x, y, (z + dz) % NZ, core))
        copy.start()
        along_z.append(copy)
    for dz in range(1, NZ):
        came = (z - dz + NZ) % NZ
        remote(
            zbuf.at[came], zbuf.at[came], z_send.at[dz], z_recv.at[dz], device(x, y, (z + dz) % NZ, core)
        ).wait_recv()
    left = lax.broadcasted_iota(jnp.int32, (PIECE, 128), 1) < ROT
    mine_block = gath.at[core, a, b]
    for zz in range(NZ):
        mine_block[zz * PIECE : (zz + 1) * PIECE, :] = zbuf[zz, :, :LAT]
    for pair in range(NZ // 2):
        mine_block[ROWS:, pair * 128 : (pair + 1) * 128] = jnp.where(
            left, zbuf[2 * pair, :, LAT:], zbuf[2 * pair + 1, :, LAT:]
        )

    sibling = device(x, y, z, 1 - core)

    def block(d, e):
        return gath.at[core, (a - d + 4) % 4, (b - e + 4) % 4]

    def along_b(e):
        return remote(mine_block, mine_block, b_send.at[e], b_recv.at[e], at_ab(a, (b + e) % 4))

    def along_a(d, e):
        return remote(block(0, e), block(0, e), a_send.at[d, e], a_recv.at[d, e], at_ab((a + d) % 4, b))

    def across(d, e):
        return remote(block(d, e), block(d, e), s_send.at[d, e], s_recv.at[d, e], sibling)

    def onward(e):
        came, to = (block(1, e), a + 1) if e in (0, 1) else (block(3, e), a + 3)
        return remote(came, came, a_send.at[2, e], a_recv.at[2, e], at_ab(to % 4, b))

    def arrived(d, e):
        came = block(d, e)
        remote(came, came, a_send.at[d, e], a_recv.at[d, e], at_ab((a + d) % 4, b)).wait_recv()

    def take(d, e):
        arrived(d, e)
        if (d, e) in ((1, 0), (1, 1), (3, 2), (3, 3)):
            onward(e).start()
        across(d, e).start()

    for e in (1, 3, 2):
        along_b(e).start()
    for e in (0, 1, 3, 2):
        if e > 0:
            came = block(0, e)
            remote(came, came, b_send.at[e], b_recv.at[e], at_ab(a, (b + e) % 4)).wait_recv()
        for d in (1, 3):
            along_a(d, e).start()
        across(0, e).start()
        if e == 3:
            take(1, 0)
            take(3, 0)

    page_row = lax.broadcasted_iota(jnp.int32, (ROWS, CHUNK), 0)

    def attend(cc, aa):
        which = cc * 4 + aa
        pick = jnp.where(drow[pl.ds(which, 1), :] == page_row, 1.0, 0.0).astype(jnp.bfloat16)
        same = (aa // 2) * 2
        order = (same, same + 1, 2 - same, 3 - same)
        for at, bb in enumerate(order):
            for zz in range(NZ):
                rot = gath[cc, aa, bb, ROWS:, (zz // 2) * 128 : (zz // 2 + 1) * 128]
                keep = left if zz % 2 == 0 else jnp.logical_not(left)
                krot[at * ROWS + zz * PIECE : at * ROWS + (zz + 1) * PIECE, :] = jnp.where(
                    keep, rot, jnp.zeros_like(rot)
                )

        def keys(count=4):
            return jnp.concatenate([gath[cc, aa, bb, :ROWS, :] for bb in order[:count]], axis=0)

        page_lat[...] += jnp.dot(pick, keys(), preferred_element_type=jnp.float32)
        page_rot[...] += jnp.dot(pick, krot[...], preferred_element_type=jnp.float32)

        nt = (((1,), (1,)), ((), ()))
        kp = kpos[pl.ds(which, 1), :]
        near = CHUNK // 2

        def logits(rows, count):
            scores = lax.dot_general(ql[rows, :], keys(count), nt, preferred_element_type=jnp.float32)
            return scores + lax.dot_general(
                qr[rows, :], krot[: count * ROWS, :], nt, preferred_element_type=jnp.float32
            )

        def fold(rows, scores, count):
            old = top[rows, :]
            new = jnp.maximum(old, jnp.max(scores, axis=1, keepdims=True))
            alpha = jnp.exp2((old - new) * LOG2E_SCALE)
            weights = jnp.exp2((scores - jnp.concatenate([new] * count, axis=1)) * LOG2E_SCALE)
            top[rows, :] = new
            summed = weights[:, :128]
            for part_at in range(1, count):
                summed += weights[:, part_at * 128 : (part_at + 1) * 128]
            den[rows, :] = den[rows, :] * alpha + summed
            mixed = jnp.dot(weights.astype(jnp.bfloat16), keys(count), preferred_element_type=jnp.float32)
            acc[rows, :] = acc[rows, :] * jnp.concatenate([alpha] * 4, axis=1) + mixed

        low_rows, high_rows = slice(0, HALF * HEADS), slice(HALF * HEADS, 2 * HALF * HEADS)
        limit = jnp.concatenate([qpos[...]] * 2, axis=1)
        high = logits(high_rows, 4)
        low = logits(low_rows, 2)
        high = jnp.concatenate(
            [high[:, :near], jnp.where(kp[:, near:] - high_at <= limit, high[:, near:], NEG)], axis=1
        )
        low = jnp.where(kp[:, :near] - low_at <= limit, low, NEG)
        fold(high_rows, high, 4)
        fold(low_rows, low, 2)

    @pl.loop(0, 4)
    def _(k):
        d = k ^ (k // 2)

        @pl.when(k == 3)
        def _():
            for e in (0, 1, 3, 2):
                arrived(2, e)
                across(2, e).start()

        attend(core, (a - d + 4) % 4)

        @pl.when(k == 0)
        def _():
            take(1, 1)
            take(3, 3)

        theirs = (b - d + 4) % 4
        for e in (0, 1, 3, 2):
            there = gath.at[1 - core, theirs, (a - e + 4) % 4]
            remote(there, there, s_send.at[d, e], s_recv.at[d, e], sibling).wait_recv()
        attend(1 - core, theirs)

        @pl.when(k == 0)
        def _():
            take(3, 2)
            take(1, 3)
            take(1, 2)
            take(3, 1)

    leaving = []
    for k in range(4):
        low_span, high_span = slice(k * ROWS, (k + 1) * ROWS), slice((k + 4) * ROWS, (k + 5) * ROWS)
        low = acc[low_span, :] / jnp.sum(den[low_span, :], axis=1, keepdims=True)
        high = acc[high_span, :] / jnp.sum(den[high_span, :], axis=1, keepdims=True)
        swap = turn[:ROWS]
        done[low_span, :] = jnp.where(swap, high, low).astype(jnp.bfloat16)
        done[high_span, :] = jnp.where(swap, low, high).astype(jnp.bfloat16)
        for at in (k, k + 4):
            span = pl.ds(at * ROWS, ROWS)
            leaving.append(pltpu.make_async_copy(done.at[span], out_hbm.at[span], out_sem.at[at]))
            leaving[-1].start()

    rotated = page_rot[:, :ROT] + page_rot[:, ROT:]
    width = LAT + ROT
    for j in range(4):
        span = slice(j * PAGES, (j + 1) * PAGES)
        paged_ref[:, j * width : j * width + LAT] = page_lat[span, :].astype(jnp.bfloat16)
        paged_ref[:, j * width + LAT : (j + 1) * width] = rotated[span, :].astype(jnp.bfloat16)

    for copy in leaving:
        copy.wait()
    for copy in scatter + along_z:
        copy.wait_send()
    for e in range(4):
        if e > 0:
            along_b(e).wait_send()
        for d in (1, 3):
            along_a(d, e).wait_send()
        onward(e).wait_send()
        for d in range(4):
            across(d, e).wait_send()


def place(attended_hbm, paged_hbm, out_hbm, paged_out_hbm, held, paged_held, in_sem, out_sem):
    pairs = []
    for k in range(8):
        span = pl.ds(k * ROWS, ROWS)
        pairs.append((attended_hbm.at[span], held.at[span], out_hbm.at[span]))
    pairs.append((paged_hbm, paged_held, paged_out_hbm))
    come = [pltpu.make_async_copy(p[0], p[1], in_sem.at[k]) for k, p in enumerate(pairs)]
    go = [pltpu.make_async_copy(p[1], p[2], out_sem.at[k]) for k, p in enumerate(pairs)]
    for copy in come:
        copy.start()
    for first, second in zip(come, go):
        first.wait()
        second.start()
    for copy in go:
        copy.wait()


def body(hidden, kv_weight, kv_gain, queries, group_order, page_owner, page_slot):
    half = ROT // 2
    freq = 10000.0 ** (-(2.0 * np.arange(half, dtype=np.float32)) / ROT)
    freq = np.tile(freq.astype(np.float32), 4)[None, :]
    bf, f32 = jnp.bfloat16, jnp.float32
    vmem = pl.BlockSpec(memory_space=pltpu.VMEM)
    hbm = pl.BlockSpec(memory_space=pl.ANY)
    smem = pl.BlockSpec(memory_space=pltpu.SMEM)
    rows = HEADS * ROWS
    dma = pltpu.SemaphoreType.DMA
    attended, paged = pl.pallas_call(
        kernel,
        out_shape=(
            jax.ShapeDtypeStruct((rows, LAT), bf),
            jax.ShapeDtypeStruct((PAGES, 4 * (LAT + ROT)), bf),
        ),
        in_specs=[hbm, hbm, vmem, vmem, hbm, smem, vmem, vmem],
        out_specs=(hbm, vmem),
        scratch_shapes=[
            pltpu.VMEM(hidden.shape, bf),
            pltpu.VMEM(kv_weight.shape[::-1], bf),
            pltpu.VMEM((HEADS, LAT + ROT, ROWS), bf),
            pltpu.VMEM((8, PIECE, LAT + ROT), f32),
            pltpu.VMEM((7, PIECE, LAT + ROT), f32),
            pltpu.VMEM((NZ, PIECE, LAT + 128), bf),
            pltpu.VMEM((2, 4, 4, BLOCK, LAT), bf),
            pltpu.VMEM((5, rows, 128), f32),
            pltpu.VMEM((rows, LAT), bf),
            pltpu.VMEM((rows, 128), bf),
            pltpu.VMEM((rows, LAT), f32),
            pltpu.VMEM((rows, 128), f32),
            pltpu.VMEM((rows, 128), f32),
            pltpu.VMEM((rows // 2, 128), jnp.int32),
            pltpu.VMEM((8, CHUNK), jnp.int32),
            pltpu.VMEM((8, CHUNK), jnp.int32),
            pltpu.VMEM((ROWS, LAT), f32),
            pltpu.VMEM((ROWS, 128), f32),
            pltpu.VMEM((CHUNK, 128), bf),
            pltpu.VMEM((rows, LAT), bf),
            dma((9,)), dma((7,)), dma((7,)), dma((8,)), dma((8,)), dma((4,)), dma((4,)), dma((4, 4)), dma((4, 4)),
            dma((4, 4)), dma((4, 4)), dma((8,)),
        ],
        name="cache_attention",
        compiler_params=pltpu.CompilerParams(
            collective_id=0, has_side_effects=True, vmem_limit_bytes=56 * 2**20
        ),
        cost_estimate=pl.CostEstimate(flops=9_000_000_000, bytes_accessed=4_000_000, transcendentals=4_000_000),
    )(
        hidden, kv_weight.T, kv_gain.reshape(1, -1), jnp.asarray(freq), queries.transpose(1, 2, 0),
        group_order, page_owner, page_slot,
    )
    attended, paged = pl.pallas_call(
        place,
        out_shape=(
            jax.ShapeDtypeStruct(attended.shape, bf),
            jax.ShapeDtypeStruct(paged.shape, bf),
        ),
        in_specs=[hbm, hbm],
        out_specs=(hbm, hbm),
        scratch_shapes=[pltpu.VMEM(attended.shape, bf), pltpu.VMEM(paged.shape, bf), dma((9,)), dma((9,))],
        compiler_params=pltpu.CompilerParams(vmem_limit_bytes=56 * 2**20),
        name="place",
    )(attended, paged)
    return attended.reshape(ROWS, HEADS, LAT), paged


def solution(mesh):
    return jax.shard_map(
        body,
        mesh=mesh,
        in_specs=(P("ctx", "dec"), P("dec", None), P(), P("ctx", "dec", None), P(), P(), P()),
        out_specs=(P("ctx", "dec", None), P("ctx", None)),
        check_vma=False,
    )
```

```python
import functools

import jax
import jax.numpy as jnp
import numpy as np
from jax import lax
from jax.experimental import pallas as pl
from jax.experimental.pallas import tpu as pltpu
from jax.sharding import PartitionSpec as P

MESH = pl.DeviceIdType.MESH
NX, NY, NZ = 4, 4, 8
HALF = 64
ROWS = 128
PIECE = 16
LAT = 512
ROT = 64
HEADS = 8
BLOCK = ROWS + PIECE
CHUNK = 4 * ROWS
PAGES = 32
EPS = 1e-6
LOG2E_SCALE = float(192.0 ** (-0.5) * np.log2(np.e))
NEG = -1e30


def device(x, y, z, core):
    return ((z * 2 + y % 2) * 2 + core, x * 2 + y // 2)


def remote(src, dst, send_sem, recv_sem, target):
    return pltpu.make_async_remote_copy(
        src_ref=src, dst_ref=dst, send_sem=send_sem, recv_sem=recv_sem, device_id=target, device_id_type=MESH
    )


def kernel(
    hidden_hbm, weight_hbm, gain_ref, freq_ref, queries_hbm, order_ref, owner_ref, slot_ref,
    out_ref, paged_ref,
    hid, wt, qt, part, sums, zbuf, gath, q32, ql, qr, acc, top, den, qpos, kpos, drow, page_lat, page_rot, krot,
    in_sem, rs_send, rs_recv, z_send, z_recv, b_send, b_recv, a_send, a_recv, s_send, s_recv,
):
    ctx = lax.axis_index("ctx")
    dec = lax.axis_index("dec")
    core = ctx % 2
    z = ctx // 4
    x = dec // 2
    y = (dec % 2) * 2 + (ctx // 2) % 2
    first = core == 0
    a = jnp.where(first, x, y)
    b = jnp.where(first, y, x)

    def at_ab(aa, bb):
        return device(jnp.where(first, aa, bb), jnp.where(first, bb, aa), z, core)

    half_me = (x // 2 + dec % 2) % 2
    sub_me = (x % 2) * 2 + dec % 2
    low_at = jnp.minimum(order_ref[ctx * 2], order_ref[ctx * 2 + 1]) * HALF
    high_at = jnp.maximum(order_ref[ctx * 2], order_ref[ctx * 2 + 1]) * HALF
    turn = jnp.full((HALF * HEADS, LAT), order_ref[ctx * 2], jnp.int32) > order_ref[ctx * 2 + 1]

    rs_offsets = [(2, 1), (1, 1), (3, 1), (2, 0), (0, 1), (1, 0), (3, 0)]

    def rs_device(dx, dy, sign):
        xx = (x + sign * dx + NX) % NX
        yh = (dec % 2 + dy) % 2
        return ctx, xx * 2 + yh

    loads = [pltpu.make_async_copy(hidden_hbm, hid, in_sem.at[0])]
    for k in range(4):
        span = pl.ds(k * 144, 144)
        loads.append(pltpu.make_async_copy(weight_hbm.at[span], wt.at[span], in_sem.at[1 + k]))
    for k in range(4):
        span = pl.ds(k * 2, 2)
        loads.append(pltpu.make_async_copy(queries_hbm.at[span], qt.at[span], in_sem.at[5 + k]))
    for load in loads:
        load.start()

    barrier = pltpu.get_barrier_semaphore()
    partners = [rs_device(dx, dy, 1) for dx, dy in rs_offsets]
    partners += [device(x, y, (z + dz) % NZ, core) for dz in range(1, NZ)]
    partners += [at_ab(a, (b + d) % 4) for d in range(1, 4)]
    partners += [at_ab((a + d) % 4, b) for d in range(1, 4)]
    partners += [device(x, y, z, 1 - core)]
    for target in partners:
        pl.semaphore_signal(barrier, inc=1, device_id=target, device_id_type=MESH)

    for load in loads[:5]:
        load.wait()
    projected = lax.dot_general(
        hid[...], wt[...], (((1,), (1,)), ((), ())), preferred_element_type=jnp.float32
    )
    upper, lower = projected[:HALF], projected[HALF:]
    swap = jnp.full(upper.shape, order_ref[ctx * 2], jnp.int32) > order_ref[ctx * 2 + 1]
    part[:4] = jnp.where(swap, lower, upper).reshape(4, PIECE, LAT + ROT)
    part[4:] = jnp.where(swap, upper, lower).reshape(4, PIECE, LAT + ROT)
    pl.semaphore_wait(barrier, len(partners))

    scatter = []
    for k, (dx, dy) in enumerate(rs_offsets):
        target = rs_device(dx, dy, 1)
        tx, ty = target[1] // 2, target[1] % 2
        theirs = ((tx // 2 + ty) % 2) * 4 + (tx % 2) * 2 + ty
        scatter.append(remote(part.at[theirs], sums.at[k], rs_send.at[k], rs_recv.at[k], target))
        scatter[-1].start()

    start_pos = jnp.where(half_me == 0, low_at, high_at) + sub_me * PIECE
    my_pos = (start_pos + lax.broadcasted_iota(jnp.int32, (PIECE, 128), 0)).astype(jnp.float32)
    angle = my_pos * freq_ref[...]
    cosine = jnp.cos(angle)
    sine = jnp.sin(angle)

    lane = lax.broadcasted_iota(jnp.int32, (1, ROWS), 1)
    lane_z = lane // PIECE
    lane_i = lane % PIECE
    mine = owner_ref[...] == ctx
    page_id = lax.broadcasted_iota(jnp.int32, (PAGES, PAGES), 1).astype(jnp.float32)
    page_of = jnp.sum(jnp.where(mine, page_id, 0.0), axis=1, keepdims=True)
    slot_of = jnp.sum(jnp.where(mine, slot_ref[...].astype(jnp.float32), 0.0), axis=1, keepdims=True)
    ctx_id = lax.broadcasted_iota(jnp.int32, (PAGES, ROWS), 0)
    ctx_lane = lax.broadcasted_iota(jnp.int32, (PAGES, ROWS), 1) // PIECE
    for cc in range(2):
        for ylo in range(2):
            picks = ctx_id == ctx_lane * 4 + (ylo * 2 + cc)
            page_z = jnp.sum(jnp.where(picks, page_of, 0.0), axis=0, keepdims=True).astype(jnp.int32)
            slot_z = jnp.sum(jnp.where(picks, slot_of, 0.0), axis=0, keepdims=True).astype(jnp.int32)
            bases = [jnp.zeros((1, ROWS), jnp.int32)] * 2
            turned = jnp.zeros((1, ROWS), jnp.int32)
            for zz in range(NZ):
                at = ((zz * 2 + ylo) * 2 + cc) * 2
                one, two = order_ref[at], order_ref[at + 1]
                bases[0] = jnp.where(lane_z == zz, jnp.minimum(one, two) * HALF, bases[0])
                bases[1] = jnp.where(lane_z == zz, jnp.maximum(one, two) * HALF, bases[1])
                turned = jnp.where(lane_z == zz, jnp.where(one > two, PAGES // 2, 0), turned)
            page_z = jnp.bitwise_xor(page_z, turned)
            for xx in range(4):
                for yhi in range(2):
                    aa, bb = (xx, yhi * 2 + ylo) if cc == 0 else (yhi * 2 + ylo, xx)
                    half, sub = (xx // 2 + yhi) % 2, (xx % 2) * 2 + yhi
                    row = (cc * 4 + aa) * 4 + bb
                    kpos[row : row + 1, :] = bases[half] + sub * PIECE + lane_i
                    page = half * (PAGES // 2) + sub * 4 + lane_i // 4
                    drow[row : row + 1, :] = jnp.where(page_z == page, (lane_i % 4) * PAGES + slot_z, -1)

    for load in loads[5:]:
        load.wait()
    rows = HEADS * ROWS
    for h in range(HEADS):
        turned = qt[h].T.astype(jnp.float32)
        turned = jnp.concatenate([turned, turned[:, LAT:]], axis=1)
        for g in range(5):
            q32[g, pl.ds(h, ROWS, stride=HEADS), :] = turned[:, g * 128 : (g + 1) * 128]
    for g in range(5):
        upper, lower = q32[g, : rows // 2, :], q32[g, rows // 2 :, :]
        swap = turn[:, :128]
        ordered = jnp.concatenate([jnp.where(swap, lower, upper), jnp.where(swap, upper, lower)], axis=0)
        if g < 4:
            ql[:, g * 128 : (g + 1) * 128] = ordered.astype(jnp.bfloat16)
        else:
            qr[...] = ordered.astype(jnp.bfloat16)
    qpos[...] = lax.broadcasted_iota(jnp.int32, qpos.shape, 0) // HEADS
    acc[...] = jnp.zeros_like(acc)
    den[...] = jnp.zeros_like(den)
    top[...] = jnp.full_like(top, NEG)
    page_lat[...] = jnp.zeros_like(page_lat)
    page_rot[...] = jnp.zeros_like(page_rot)

    total = part[half_me * 4 + sub_me]
    for k, copy in enumerate(scatter):
        copy.wait_recv()
        total = total + sums[k]

    latent = total[:, :LAT]
    inverse = lax.rsqrt(jnp.mean(latent * latent, axis=1, keepdims=True) + EPS)
    latent = latent * inverse * gain_ref[...]
    half = ROT // 2
    r1, r2 = total[:, LAT : LAT + half], total[:, LAT + half :]
    c1, s1 = cosine[:, :half], sine[:, :half]
    turned = jnp.concatenate([r1 * c1 - r2 * s1, r1 * s1 + r2 * c1], axis=1)
    zbuf[z] = jnp.concatenate([latent, turned, turned], axis=1).astype(jnp.bfloat16)

    along_z = []
    for dz in (4, 3, 5, 2, 6, 1, 7):
        copy = remote(zbuf.at[z], zbuf.at[z], z_send.at[dz], z_recv.at[dz], device(x, y, (z + dz) % NZ, core))
        copy.start()
        along_z.append(copy)
    for dz in range(1, NZ):
        came = (z - dz + NZ) % NZ
        remote(
            zbuf.at[came], zbuf.at[came], z_send.at[dz], z_recv.at[dz], device(x, y, (z + dz) % NZ, core)
        ).wait_recv()
    left = lax.broadcasted_iota(jnp.int32, (PIECE, 128), 1) < ROT
    mine_block = gath.at[core, a, b]
    for zz in range(NZ):
        mine_block[zz * PIECE : (zz + 1) * PIECE, :] = zbuf[zz, :, :LAT]
    for pair in range(NZ // 2):
        mine_block[ROWS:, pair * 128 : (pair + 1) * 128] = jnp.where(
            left, zbuf[2 * pair, :, LAT:], zbuf[2 * pair + 1, :, LAT:]
        )

    sibling = device(x, y, z, 1 - core)

    def block(d, e):
        return gath.at[core, (a - d + 4) % 4, (b - e + 4) % 4]

    def along_b(e):
        return remote(mine_block, mine_block, b_send.at[e], b_recv.at[e], at_ab(a, (b + e) % 4))

    def along_a(d, e):
        return remote(block(0, e), block(0, e), a_send.at[d, e], a_recv.at[d, e], at_ab((a + d) % 4, b))

    def across(d, e):
        return remote(block(d, e), block(d, e), s_send.at[d, e], s_recv.at[d, e], sibling)

    def onward(e):
        came, to = (block(1, e), a + 1) if e in (0, 1) else (block(3, e), a + 3)
        return remote(came, came, a_send.at[2, e], a_recv.at[2, e], at_ab(to % 4, b))

    def arrived(d, e):
        came = block(d, e)
        remote(came, came, a_send.at[d, e], a_recv.at[d, e], at_ab((a + d) % 4, b)).wait_recv()

    def take(d, e):
        arrived(d, e)
        if (d, e) in ((1, 0), (1, 1), (3, 2), (3, 3)):
            onward(e).start()
        across(d, e).start()

    for e in (1, 3, 2):
        along_b(e).start()
    for e in (0, 1, 3, 2):
        if e > 0:
            came = block(0, e)
            remote(came, came, b_send.at[e], b_recv.at[e], at_ab(a, (b + e) % 4)).wait_recv()
        for d in (1, 3):
            along_a(d, e).start()
        across(0, e).start()
        if e == 3:
            take(1, 0)
            take(3, 0)

    page_row = lax.broadcasted_iota(jnp.int32, (ROWS, CHUNK), 0)

    def attend(cc, pa, pb, k):
        near = jnp.logical_or(k == 1, k == 2)
        strip = (pa + jnp.where(k == 3, 2, 0)) % 4
        order = []
        for at in range(4):
            bb_near = (pb - 2 * (k - 1) - at % 2 + 8) % 4
            half = bb_near // 2 if at < 2 else 1 - bb_near // 2
            aa_near = half * 2 + (pa + 1) % 2
            bb_strip = (strip // 2 if at < 2 else 1 - strip // 2) * 2 + at % 2
            order.append((jnp.where(near, aa_near, strip), jnp.where(near, bb_near, bb_strip)))
        which = [(cc * 4 + aa) * 4 + bb for aa, bb in order]
        row_of = jnp.concatenate([drow[pl.ds(w, 1), :] for w in which], axis=1)
        pick = jnp.where(row_of == page_row, 1.0, 0.0).astype(jnp.bfloat16)
        for at, (aa, bb) in enumerate(order):
            for zz in range(NZ):
                rot = gath[cc, aa, bb, ROWS:, (zz // 2) * 128 : (zz // 2 + 1) * 128]
                keep = left if zz % 2 == 0 else jnp.logical_not(left)
                krot[at * ROWS + zz * PIECE : at * ROWS + (zz + 1) * PIECE, :] = jnp.where(
                    keep, rot, jnp.zeros_like(rot)
                )

        def keys(count=4):
            return jnp.concatenate([gath[cc, aa, bb, :ROWS, :] for aa, bb in order[:count]], axis=0)

        page_lat[...] += jnp.dot(pick, keys(), preferred_element_type=jnp.float32)
        page_rot[...] += jnp.dot(pick, krot[...], preferred_element_type=jnp.float32)

        nt = (((1,), (1,)), ((), ()))
        kp = jnp.concatenate([kpos[pl.ds(w, 1), :] for w in which], axis=1)
        near = CHUNK // 2

        def logits(rows, count):
            scores = lax.dot_general(ql[rows, :], keys(count), nt, preferred_element_type=jnp.float32)
            return scores + lax.dot_general(
                qr[rows, :], krot[: count * ROWS, :], nt, preferred_element_type=jnp.float32
            )

        def fold(rows, scores, count):
            old = top[rows, :]
            new = jnp.maximum(old, jnp.max(scores, axis=1, keepdims=True))
            alpha = jnp.exp2((old - new) * LOG2E_SCALE)
            weights = jnp.exp2((scores - jnp.concatenate([new] * count, axis=1)) * LOG2E_SCALE)
            top[rows, :] = new
            summed = weights[:, :128]
            for part_at in range(1, count):
                summed += weights[:, part_at * 128 : (part_at + 1) * 128]
            den[rows, :] = den[rows, :] * alpha + summed
            mixed = jnp.dot(weights.astype(jnp.bfloat16), keys(count), preferred_element_type=jnp.float32)
            acc[rows, :] = acc[rows, :] * jnp.concatenate([alpha] * 4, axis=1) + mixed

        low_rows, high_rows = slice(0, HALF * HEADS), slice(HALF * HEADS, 2 * HALF * HEADS)
        limit = jnp.concatenate([qpos[...]] * 2, axis=1)
        high = logits(high_rows, 4)
        low = logits(low_rows, 2)
        high = jnp.concatenate(
            [high[:, :near], jnp.where(kp[:, near:] - high_at <= limit, high[:, near:], NEG)], axis=1
        )
        low = jnp.where(kp[:, :near] - low_at <= limit, low, NEG)
        fold(high_rows, high, 4)
        fold(low_rows, low, 2)

    @pl.loop(0, 4)
    def _(k):
        @pl.when(k == 3)
        def _():
            for e in (3, 2):
                arrived(2, e)
                across(2, e).start()

        attend(core, a, b, k)

        @pl.when(k == 0)
        def _():
            for d, e in ((1, 1), (3, 1), (3, 3), (1, 3)):
                take(d, e)

        @pl.when(k == 1)
        def _():
            for d, e in ((3, 2), (1, 2)):
                take(d, e)

        @pl.when(k == 2)
        def _():
            for e in (0, 1):
                arrived(2, e)
                across(2, e).start()

        near = jnp.logical_or(k == 1, k == 2)
        for at in range(4):
            d = jnp.where(near, 1 + 2 * (at % 2), jnp.where(k == 3, 2, 0))
            e = jnp.where(near, jnp.where(k == 1, at // 2, 3 - at // 2), at)
            there = gath.at[1 - core, (b - d + 4) % 4, (a - e + 4) % 4]
            remote(there, there, s_send.at[d, e], s_recv.at[d, e], sibling).wait_recv()
        attend(1 - core, b, a, k)

    for k in range(4):
        low_span, high_span = slice(k * ROWS, (k + 1) * ROWS), slice((k + 4) * ROWS, (k + 5) * ROWS)
        low = acc[low_span, :] / jnp.sum(den[low_span, :], axis=1, keepdims=True)
        high = acc[high_span, :] / jnp.sum(den[high_span, :], axis=1, keepdims=True)
        swap = turn[:ROWS]
        out_ref[low_span, :] = jnp.where(swap, high, low).astype(jnp.bfloat16)
        out_ref[high_span, :] = jnp.where(swap, low, high).astype(jnp.bfloat16)

    rotated = page_rot[:, :ROT] + page_rot[:, ROT:]
    width = LAT + ROT
    for j in range(4):
        span = slice(j * PAGES, (j + 1) * PAGES)
        paged_ref[:, j * width : j * width + LAT] = page_lat[span, :].astype(jnp.bfloat16)
        paged_ref[:, j * width + LAT : (j + 1) * width] = rotated[span, :].astype(jnp.bfloat16)

    for copy in scatter + along_z:
        copy.wait_send()
    for e in range(4):
        if e > 0:
            along_b(e).wait_send()
        for d in (1, 3):
            along_a(d, e).wait_send()
        onward(e).wait_send()
        for d in range(4):
            across(d, e).wait_send()


def body(hidden, kv_weight, kv_gain, queries, group_order, page_owner, page_slot):
    half = ROT // 2
    freq = 10000.0 ** (-(2.0 * np.arange(half, dtype=np.float32)) / ROT)
    freq = np.tile(freq.astype(np.float32), 4)[None, :]
    bf, f32 = jnp.bfloat16, jnp.float32
    vmem = pl.BlockSpec(memory_space=pltpu.VMEM)
    hbm = pl.BlockSpec(memory_space=pl.ANY)
    smem = pl.BlockSpec(memory_space=pltpu.SMEM)
    rows = HEADS * ROWS
    dma = pltpu.SemaphoreType.DMA
    attended, paged = pl.pallas_call(
        kernel,
        out_shape=(
            pltpu.VMEM((rows, LAT), bf),
            pltpu.VMEM((PAGES, 4 * (LAT + ROT)), bf),
        ),
        in_specs=[hbm, hbm, vmem, vmem, hbm, smem, vmem, vmem],
        out_specs=(vmem, vmem),
        scratch_shapes=[
            pltpu.VMEM(hidden.shape, bf),
            pltpu.VMEM(kv_weight.shape[::-1], bf),
            pltpu.VMEM((HEADS, LAT + ROT, ROWS), bf),
            pltpu.VMEM((8, PIECE, LAT + ROT), f32),
            pltpu.VMEM((7, PIECE, LAT + ROT), f32),
            pltpu.VMEM((NZ, PIECE, LAT + 128), bf),
            pltpu.VMEM((2, 4, 4, BLOCK, LAT), bf),
            pltpu.VMEM((5, rows, 128), f32),
            pltpu.VMEM((rows, LAT), bf),
            pltpu.VMEM((rows, 128), bf),
            pltpu.VMEM((rows, LAT), f32),
            pltpu.VMEM((rows, 128), f32),
            pltpu.VMEM((rows, 128), f32),
            pltpu.VMEM((rows // 2, 128), jnp.int32),
            pltpu.VMEM((32, ROWS), jnp.int32),
            pltpu.VMEM((32, ROWS), jnp.int32),
            pltpu.VMEM((ROWS, LAT), f32),
            pltpu.VMEM((ROWS, 128), f32),
            pltpu.VMEM((CHUNK, 128), bf),
            dma((9,)), dma((7,)), dma((7,)), dma((8,)), dma((8,)), dma((4,)), dma((4,)), dma((4, 4)), dma((4, 4)),
            dma((4, 4)), dma((4, 4)),
        ],
        name="cache_attention",
        compiler_params=pltpu.CompilerParams(
            collective_id=0, has_side_effects=True, vmem_limit_bytes=56 * 2**20
        ),
        cost_estimate=pl.CostEstimate(flops=9_000_000_000, bytes_accessed=4_000_000, transcendentals=4_000_000),
    )(
        hidden, kv_weight.T, kv_gain.reshape(1, -1), jnp.asarray(freq), queries.transpose(1, 2, 0),
        group_order, page_owner, page_slot,
    )
    return attended.reshape(ROWS, HEADS, LAT), paged


def solution(mesh):
    return jax.shard_map(
        body,
        mesh=mesh,
        in_specs=(P("ctx", "dec"), P("dec", None), P(), P("ctx", "dec", None), P(), P(), P()),
        out_specs=(P("ctx", "dec", None), P("ctx", None)),
        check_vma=False,
    )
```

```python
import functools

import jax
import jax.numpy as jnp
import numpy as np
from jax import lax
from jax.experimental import pallas as pl
from jax.experimental.pallas import tpu as pltpu
from jax.sharding import PartitionSpec as P

MESH = pl.DeviceIdType.MESH
NX, NY, NZ = 4, 4, 8
HALF = 64
ROWS = 128
PIECE = 16
LAT = 512
ROT = 64
HEADS = 8
BLOCK = ROWS + PIECE
CHUNK = 4 * ROWS
PAGES = 32
EPS = 1e-6
LOG2E_SCALE = float(192.0 ** (-0.5) * np.log2(np.e))
NEG = -1e30
STEPS = (0, 1, 7, 2, 6, 3, 5, 4)
EARLY = ROWS // 2


def device(x, y, z, core):
    return ((z * 2 + y % 2) * 2 + core, x * 2 + y // 2)


def remote(src, dst, send_sem, recv_sem, target):
    return pltpu.make_async_remote_copy(
        src_ref=src, dst_ref=dst, send_sem=send_sem, recv_sem=recv_sem, device_id=target, device_id_type=MESH
    )


def kernel(
    hidden_hbm, weight_hbm, gain_ref, freq_ref, queries_hbm, order_ref, owner_ref, slot_ref,
    out_ref, paged_ref,
    hid, wt, qt, part, sums, zbuf, gath, q32, ql, qr, acc, top, den, qpos, kpos, drow, page_lat, page_rot, krot,
    in_sem, rs_send, rs_recv, z_send, z_recv, b_send, b_recv, a_send, a_recv, s_send, s_recv,
):
    ctx = lax.axis_index("ctx")
    dec = lax.axis_index("dec")
    core = ctx % 2
    z = ctx // 4
    x = dec // 2
    y = (dec % 2) * 2 + (ctx // 2) % 2
    first = core == 0
    a = jnp.where(first, x, y)
    b = jnp.where(first, y, x)

    def at_ab(aa, bb):
        return device(jnp.where(first, aa, bb), jnp.where(first, bb, aa), z, core)

    half_me = (x // 2 + dec % 2) % 2
    sub_me = (x % 2) * 2 + dec % 2
    low_at = jnp.minimum(order_ref[ctx * 2], order_ref[ctx * 2 + 1]) * HALF
    high_at = jnp.maximum(order_ref[ctx * 2], order_ref[ctx * 2 + 1]) * HALF
    turn = jnp.full((HALF * HEADS, LAT), order_ref[ctx * 2], jnp.int32) > order_ref[ctx * 2 + 1]

    rs_offsets = [(2, 1), (1, 1), (3, 1), (2, 0), (0, 1), (1, 0), (3, 0)]

    def rs_device(dx, dy, sign):
        xx = (x + sign * dx + NX) % NX
        yh = (dec % 2 + dy) % 2
        return ctx, xx * 2 + yh

    loads = [pltpu.make_async_copy(hidden_hbm, hid, in_sem.at[0])]
    for k in range(4):
        span = pl.ds(k * 144, 144)
        loads.append(pltpu.make_async_copy(weight_hbm.at[span], wt.at[span], in_sem.at[1 + k]))
    for k in range(4):
        span = pl.ds(k * 2, 2)
        loads.append(pltpu.make_async_copy(queries_hbm.at[span], qt.at[span], in_sem.at[5 + k]))
    for load in loads:
        load.start()

    barrier = pltpu.get_barrier_semaphore()
    partners = [rs_device(dx, dy, 1) for dx, dy in rs_offsets]
    partners += [device(x, y, (z + dz) % NZ, core) for dz in range(1, NZ)]
    partners += [at_ab(a, (b + d) % 4) for d in range(1, 4)]
    partners += [at_ab((a + d) % 4, b) for d in range(1, 4)]
    partners += [device(x, y, z, 1 - core)]
    for target in partners:
        pl.semaphore_signal(barrier, inc=1, device_id=target, device_id_type=MESH)

    for load in loads[:5]:
        load.wait()
    projected = lax.dot_general(
        hid[...], wt[...], (((1,), (1,)), ((), ())), preferred_element_type=jnp.float32
    )
    upper, lower = projected[:HALF], projected[HALF:]
    swap = jnp.full(upper.shape, order_ref[ctx * 2], jnp.int32) > order_ref[ctx * 2 + 1]
    part[:4] = jnp.where(swap, lower, upper).reshape(4, PIECE, LAT + ROT)
    part[4:] = jnp.where(swap, upper, lower).reshape(4, PIECE, LAT + ROT)
    pl.semaphore_wait(barrier, len(partners))

    scatter = []
    for k, (dx, dy) in enumerate(rs_offsets):
        target = rs_device(dx, dy, 1)
        tx, ty = target[1] // 2, target[1] % 2
        theirs = ((tx // 2 + ty) % 2) * 4 + (tx % 2) * 2 + ty
        scatter.append(remote(part.at[theirs], sums.at[k], rs_send.at[k], rs_recv.at[k], target))
        scatter[-1].start()

    start_pos = jnp.where(half_me == 0, low_at, high_at) + sub_me * PIECE
    my_pos = (start_pos + lax.broadcasted_iota(jnp.int32, (PIECE, 128), 0)).astype(jnp.float32)
    angle = my_pos * freq_ref[...]
    cosine = jnp.cos(angle)
    sine = jnp.sin(angle)

    lane = lax.broadcasted_iota(jnp.int32, (1, ROWS), 1)
    lane_z = lane // PIECE
    lane_i = lane % PIECE
    mine = owner_ref[...] == ctx
    page_id = lax.broadcasted_iota(jnp.int32, (PAGES, PAGES), 1).astype(jnp.float32)
    page_of = jnp.sum(jnp.where(mine, page_id, 0.0), axis=1, keepdims=True)
    slot_of = jnp.sum(jnp.where(mine, slot_ref[...].astype(jnp.float32), 0.0), axis=1, keepdims=True)
    ctx_id = lax.broadcasted_iota(jnp.int32, (PAGES, ROWS), 0)
    place_lane = lax.broadcasted_iota(jnp.int32, (PAGES, ROWS), 1) // PIECE
    ctx_lane = jnp.zeros((PAGES, ROWS), jnp.int32)
    for at, step in enumerate(STEPS):
        ctx_lane = jnp.where(place_lane == at, (z + step) % NZ, ctx_lane)
    for cc in range(2):
        for ylo in range(2):
            picks = ctx_id == ctx_lane * 4 + (ylo * 2 + cc)
            page_z = jnp.sum(jnp.where(picks, page_of, 0.0), axis=0, keepdims=True).astype(jnp.int32)
            slot_z = jnp.sum(jnp.where(picks, slot_of, 0.0), axis=0, keepdims=True).astype(jnp.int32)
            bases = [jnp.zeros((1, ROWS), jnp.int32)] * 2
            turned = jnp.zeros((1, ROWS), jnp.int32)
            for zz, step in enumerate(STEPS):
                at = (((z + step) % NZ * 2 + ylo) * 2 + cc) * 2
                one, two = order_ref[at], order_ref[at + 1]
                bases[0] = jnp.where(lane_z == zz, jnp.minimum(one, two) * HALF, bases[0])
                bases[1] = jnp.where(lane_z == zz, jnp.maximum(one, two) * HALF, bases[1])
                turned = jnp.where(lane_z == zz, jnp.where(one > two, PAGES // 2, 0), turned)
            page_z = jnp.bitwise_xor(page_z, turned)
            for xx in range(4):
                for yhi in range(2):
                    aa, bb = (xx, yhi * 2 + ylo) if cc == 0 else (yhi * 2 + ylo, xx)
                    half, sub = (xx // 2 + yhi) % 2, (xx % 2) * 2 + yhi
                    row = (cc * 4 + aa) * 4 + bb
                    kpos[row : row + 1, :] = bases[half] + sub * PIECE + lane_i
                    page = half * (PAGES // 2) + sub * 4 + lane_i // 4
                    drow[row : row + 1, :] = jnp.where(page_z == page, (lane_i % 4) * PAGES + slot_z, -1)

    for load in loads[5:]:
        load.wait()
    rows = HEADS * ROWS
    for h in range(HEADS):
        turned = qt[h].T.astype(jnp.float32)
        turned = jnp.concatenate([turned, turned[:, LAT:]], axis=1)
        for g in range(5):
            q32[g, pl.ds(h, ROWS, stride=HEADS), :] = turned[:, g * 128 : (g + 1) * 128]
    for g in range(5):
        upper, lower = q32[g, : rows // 2, :], q32[g, rows // 2 :, :]
        swap = turn[:, :128]
        ordered = jnp.concatenate([jnp.where(swap, lower, upper), jnp.where(swap, upper, lower)], axis=0)
        if g < 4:
            ql[:, g * 128 : (g + 1) * 128] = ordered.astype(jnp.bfloat16)
        else:
            qr[...] = ordered.astype(jnp.bfloat16)
    qpos[...] = lax.broadcasted_iota(jnp.int32, qpos.shape, 0) // HEADS
    acc[...] = jnp.zeros_like(acc)
    den[...] = jnp.zeros_like(den)
    top[...] = jnp.full_like(top, NEG)
    page_lat[...] = jnp.zeros_like(page_lat)
    page_rot[...] = jnp.zeros_like(page_rot)

    total = part[half_me * 4 + sub_me]
    for k, copy in enumerate(scatter):
        copy.wait_recv()
        total = total + sums[k]

    latent = total[:, :LAT]
    inverse = lax.rsqrt(jnp.mean(latent * latent, axis=1, keepdims=True) + EPS)
    latent = latent * inverse * gain_ref[...]
    half = ROT // 2
    r1, r2 = total[:, LAT : LAT + half], total[:, LAT + half :]
    c1, s1 = cosine[:, :half], sine[:, :half]
    turned = jnp.concatenate([r1 * c1 - r2 * s1, r1 * s1 + r2 * c1], axis=1)
    zbuf[z] = jnp.concatenate([latent, turned, turned], axis=1).astype(jnp.bfloat16)

    along_z = []
    for dz in (7, 1, 6, 4, 3, 5, 2):
        copy = remote(zbuf.at[z], zbuf.at[z], z_send.at[dz], z_recv.at[dz], device(x, y, (z + dz) % NZ, core))
        copy.start()
        along_z.append(copy)
    left = lax.broadcasted_iota(jnp.int32, (PIECE, 128), 1) < ROT
    mine_block = gath.at[core, a, b]

    def settle(places):
        for at in places:
            came = (z + STEPS[at]) % NZ
            dz = (NZ - STEPS[at]) % NZ
            if dz > 0:
                remote(
                    zbuf.at[came], zbuf.at[came], z_send.at[dz], z_recv.at[dz], device(x, y, (z + dz) % NZ, core)
                ).wait_recv()
        for at in places:
            mine_block[at * PIECE : (at + 1) * PIECE, :] = zbuf[(z + STEPS[at]) % NZ, :, :LAT]

    sibling = device(x, y, z, 1 - core)

    def block(d, e):
        return gath.at[core, (a - d + 4) % 4, (b - e + 4) % 4]

    def some(ref, h):
        return ref.at[pl.ds(0, EARLY)] if h == 0 else ref.at[pl.ds(EARLY, BLOCK - EARLY)]

    def along_b(e, h):
        return remote(some(mine_block, h), some(mine_block, h), b_send.at[e, h], b_recv.at[e, h], at_ab(a, (b + e) % 4))

    def own_along_a(d, h):
        col = 4 * (1 - h)
        return remote(
            some(mine_block, h), some(mine_block, h), a_send.at[d, col], a_recv.at[d, col], at_ab((a + d) % 4, b)
        )

    def along_a(d, e):
        return remote(block(0, e), block(0, e), a_send.at[d, e], a_recv.at[d, e], at_ab((a + d) % 4, b))

    def across(d, e):
        return remote(block(d, e), block(d, e), s_send.at[d, e], s_recv.at[d, e], sibling)

    def onward(e):
        came, to = (block(1, e), a + 1) if e in (0, 1) else (block(3, e), a + 3)
        return remote(came, came, a_send.at[2, e], a_recv.at[2, e], at_ab(to % 4, b))

    def arrived(d, e):
        came = block(d, e)
        if e == 0 and d != 2:
            for h in range(2):
                col = 4 * (1 - h)
                remote(
                    some(came, h), some(came, h), a_send.at[d, col], a_recv.at[d, col], at_ab((a + d) % 4, b)
                ).wait_recv()
        else:
            remote(came, came, a_send.at[d, e], a_recv.at[d, e], at_ab((a + d) % 4, b)).wait_recv()

    def take(d, e):
        arrived(d, e)
        if (d, e) in ((1, 0), (1, 1), (3, 2), (3, 3)):
            onward(e).start()
        across(d, e).start()

    for h in range(2):
        settle(range(4 * h, 4 * h + 4))
        if h == 1:
            for pair in range(NZ // 2):
                mine_block[ROWS:, pair * 128 : (pair + 1) * 128] = jnp.where(
                    left,
                    zbuf[(z + STEPS[2 * pair]) % NZ, :, LAT:],
                    zbuf[(z + STEPS[2 * pair + 1]) % NZ, :, LAT:],
                )
        for e in (1, 3, 2):
            along_b(e, h).start()
        for d in (1, 3):
            own_along_a(d, h).start()
    for e in (0, 1, 3, 2):
        if e > 0:
            for h in range(2):
                came = some(block(0, e), h)
                remote(came, came, b_send.at[e, h], b_recv.at[e, h], at_ab(a, (b + e) % 4)).wait_recv()
            for d in (1, 3):
                along_a(d, e).start()
        across(0, e).start()
        if e == 3:
            take(1, 0)
            take(3, 0)

    page_row = lax.broadcasted_iota(jnp.int32, (ROWS, CHUNK), 0)

    def attend(cc, pa, pb, k):
        near = jnp.logical_or(k == 1, k == 2)
        strip = (pa + jnp.where(k == 3, 2, 0)) % 4
        order = []
        for at in range(4):
            bb_near = (pb - 2 * (k - 1) - at % 2 + 8) % 4
            half = bb_near // 2 if at < 2 else 1 - bb_near // 2
            aa_near = half * 2 + (pa + 1) % 2
            bb_strip = (strip // 2 if at < 2 else 1 - strip // 2) * 2 + at % 2
            order.append((jnp.where(near, aa_near, strip), jnp.where(near, bb_near, bb_strip)))
        which = [(cc * 4 + aa) * 4 + bb for aa, bb in order]
        row_of = jnp.concatenate([drow[pl.ds(w, 1), :] for w in which], axis=1)
        pick = jnp.where(row_of == page_row, 1.0, 0.0).astype(jnp.bfloat16)
        for at, (aa, bb) in enumerate(order):
            for zz in range(NZ):
                rot = gath[cc, aa, bb, ROWS:, (zz // 2) * 128 : (zz // 2 + 1) * 128]
                keep = left if zz % 2 == 0 else jnp.logical_not(left)
                krot[at * ROWS + zz * PIECE : at * ROWS + (zz + 1) * PIECE, :] = jnp.where(
                    keep, rot, jnp.zeros_like(rot)
                )

        def keys(count=4):
            return jnp.concatenate([gath[cc, aa, bb, :ROWS, :] for aa, bb in order[:count]], axis=0)

        page_lat[...] += jnp.dot(pick, keys(), preferred_element_type=jnp.float32)
        page_rot[...] += jnp.dot(pick, krot[...], preferred_element_type=jnp.float32)

        nt = (((1,), (1,)), ((), ()))
        kp = jnp.concatenate([kpos[pl.ds(w, 1), :] for w in which], axis=1)
        near = CHUNK // 2

        def logits(rows, count):
            scores = lax.dot_general(ql[rows, :], keys(count), nt, preferred_element_type=jnp.float32)
            return scores + lax.dot_general(
                qr[rows, :], krot[: count * ROWS, :], nt, preferred_element_type=jnp.float32
            )

        def fold(rows, scores, count):
            old = top[rows, :]
            new = jnp.maximum(old, jnp.max(scores, axis=1, keepdims=True))
            alpha = jnp.exp2((old - new) * LOG2E_SCALE)
            weights = jnp.exp2((scores - jnp.concatenate([new] * count, axis=1)) * LOG2E_SCALE)
            top[rows, :] = new
            summed = weights[:, :128]
            for part_at in range(1, count):
                summed += weights[:, part_at * 128 : (part_at + 1) * 128]
            den[rows, :] = den[rows, :] * alpha + summed
            mixed = jnp.dot(weights.astype(jnp.bfloat16), keys(count), preferred_element_type=jnp.float32)
            acc[rows, :] = acc[rows, :] * jnp.concatenate([alpha] * 4, axis=1) + mixed

        low_rows, high_rows = slice(0, HALF * HEADS), slice(HALF * HEADS, 2 * HALF * HEADS)
        limit = jnp.concatenate([qpos[...]] * 2, axis=1)
        high = logits(high_rows, 4)
        low = logits(low_rows, 2)
        high = jnp.concatenate(
            [high[:, :near], jnp.where(kp[:, near:] - high_at <= limit, high[:, near:], NEG)], axis=1
        )
        low = jnp.where(kp[:, :near] - low_at <= limit, low, NEG)
        fold(high_rows, high, 4)
        fold(low_rows, low, 2)

    @pl.loop(0, 4)
    def _(k):
        @pl.when(k == 3)
        def _():
            for e in (3, 2):
                arrived(2, e)
                across(2, e).start()

        attend(core, a, b, k)

        @pl.when(k == 0)
        def _():
            for d, e in ((1, 1), (3, 1), (3, 3), (1, 3)):
                take(d, e)

        @pl.when(k == 1)
        def _():
            for d, e in ((3, 2), (1, 2)):
                take(d, e)

        @pl.when(k == 2)
        def _():
            for e in (0, 1):
                arrived(2, e)
                across(2, e).start()

        near = jnp.logical_or(k == 1, k == 2)
        for at in range(4):
            d = jnp.where(near, 1 + 2 * (at % 2), jnp.where(k == 3, 2, 0))
            e = jnp.where(near, jnp.where(k == 1, at // 2, 3 - at // 2), at)
            there = gath.at[1 - core, (b - d + 4) % 4, (a - e + 4) % 4]
            remote(there, there, s_send.at[d, e], s_recv.at[d, e], sibling).wait_recv()
        attend(1 - core, b, a, k)

    for k in range(4):
        low_span, high_span = slice(k * ROWS, (k + 1) * ROWS), slice((k + 4) * ROWS, (k + 5) * ROWS)
        low = acc[low_span, :] / jnp.sum(den[low_span, :], axis=1, keepdims=True)
        high = acc[high_span, :] / jnp.sum(den[high_span, :], axis=1, keepdims=True)
        swap = turn[:ROWS]
        out_ref[low_span, :] = jnp.where(swap, high, low).astype(jnp.bfloat16)
        out_ref[high_span, :] = jnp.where(swap, low, high).astype(jnp.bfloat16)

    rotated = page_rot[:, :ROT] + page_rot[:, ROT:]
    width = LAT + ROT
    for j in range(4):
        span = slice(j * PAGES, (j + 1) * PAGES)
        paged_ref[:, j * width : j * width + LAT] = page_lat[span, :].astype(jnp.bfloat16)
        paged_ref[:, j * width + LAT : (j + 1) * width] = rotated[span, :].astype(jnp.bfloat16)

    for copy in scatter + along_z:
        copy.wait_send()
    for e in range(4):
        if e > 0:
            for h in range(2):
                along_b(e, h).wait_send()
        for d in (1, 3):
            if e > 0:
                along_a(d, e).wait_send()
            else:
                own_along_a(d, 0).wait_send()
                own_along_a(d, 1).wait_send()
        onward(e).wait_send()
        for d in range(4):
            across(d, e).wait_send()


def body(hidden, kv_weight, kv_gain, queries, group_order, page_owner, page_slot):
    half = ROT // 2
    freq = 10000.0 ** (-(2.0 * np.arange(half, dtype=np.float32)) / ROT)
    freq = np.tile(freq.astype(np.float32), 4)[None, :]
    bf, f32 = jnp.bfloat16, jnp.float32
    vmem = pl.BlockSpec(memory_space=pltpu.VMEM)
    hbm = pl.BlockSpec(memory_space=pl.ANY)
    smem = pl.BlockSpec(memory_space=pltpu.SMEM)
    rows = HEADS * ROWS
    dma = pltpu.SemaphoreType.DMA
    attended, paged = pl.pallas_call(
        kernel,
        out_shape=(
            pltpu.VMEM((rows, LAT), bf),
            pltpu.VMEM((PAGES, 4 * (LAT + ROT)), bf),
        ),
        in_specs=[hbm, hbm, vmem, vmem, hbm, smem, vmem, vmem],
        out_specs=(vmem, vmem),
        scratch_shapes=[
            pltpu.VMEM(hidden.shape, bf),
            pltpu.VMEM(kv_weight.shape[::-1], bf),
            pltpu.VMEM((HEADS, LAT + ROT, ROWS), bf),
            pltpu.VMEM((8, PIECE, LAT + ROT), f32),
            pltpu.VMEM((7, PIECE, LAT + ROT), f32),
            pltpu.VMEM((NZ, PIECE, LAT + 128), bf),
            pltpu.VMEM((2, 4, 4, BLOCK, LAT), bf),
            pltpu.VMEM((5, rows, 128), f32),
            pltpu.VMEM((rows, LAT), bf),
            pltpu.VMEM((rows, 128), bf),
            pltpu.VMEM((rows, LAT), f32),
            pltpu.VMEM((rows, 128), f32),
            pltpu.VMEM((rows, 128), f32),
            pltpu.VMEM((rows // 2, 128), jnp.int32),
            pltpu.VMEM((32, ROWS), jnp.int32),
            pltpu.VMEM((32, ROWS), jnp.int32),
            pltpu.VMEM((ROWS, LAT), f32),
            pltpu.VMEM((ROWS, 128), f32),
            pltpu.VMEM((CHUNK, 128), bf),
            dma((9,)), dma((7,)), dma((7,)), dma((8,)), dma((8,)), dma((4, 2)), dma((4, 2)), dma((4, 5)), dma((4, 5)),
            dma((4, 4)), dma((4, 4)),
        ],
        name="cache_attention",
        compiler_params=pltpu.CompilerParams(
            collective_id=0, has_side_effects=True, vmem_limit_bytes=56 * 2**20
        ),
        cost_estimate=pl.CostEstimate(flops=9_000_000_000, bytes_accessed=4_000_000, transcendentals=4_000_000),
    )(
        hidden, kv_weight.T, kv_gain.reshape(1, -1), jnp.asarray(freq), queries.transpose(1, 2, 0),
        group_order, page_owner, page_slot,
    )
    return attended.reshape(ROWS, HEADS, LAT), paged


def solution(mesh):
    return jax.shard_map(
        body,
        mesh=mesh,
        in_specs=(P("ctx", "dec"), P("dec", None), P(), P("ctx", "dec", None), P(), P(), P()),
        out_specs=(P("ctx", "dec", None), P("ctx", None)),
        check_vma=False,
    )
```

```python
import functools

import jax
import jax.numpy as jnp
import numpy as np
from jax import lax
from jax.experimental import pallas as pl
from jax.experimental.pallas import tpu as pltpu
from jax.sharding import PartitionSpec as P

MESH = pl.DeviceIdType.MESH
NX, NY, NZ = 4, 4, 8
HALF = 64
ROWS = 128
PIECE = 16
LAT = 512
ROT = 64
HEADS = 8
BLOCK = ROWS + PIECE
CHUNK = 4 * ROWS
PAGES = 32
EPS = 1e-6
LOG2E_SCALE = float(192.0 ** (-0.5) * np.log2(np.e))
NEG = -1e30
STEPS = (0, 1, 7, 2, 6, 3, 5, 4)
EARLY = ROWS // 2


def device(x, y, z, core):
    return ((z * 2 + y % 2) * 2 + core, x * 2 + y // 2)


def remote(src, dst, send_sem, recv_sem, target):
    return pltpu.make_async_remote_copy(
        src_ref=src, dst_ref=dst, send_sem=send_sem, recv_sem=recv_sem, device_id=target, device_id_type=MESH
    )


def kernel(
    hidden_hbm, weight_hbm, gain_ref, freq_ref, queries_hbm, order_ref, owner_ref, slot_ref,
    out_ref, paged_ref,
    hid, wt, qt, part, sums, zbuf, gath, q32, ql, qr, acc, top, den, qpos, kpos, drow, page_lat, page_rot, krot,
    in_sem, rs_send, rs_recv, z_send, z_recv, b_send, b_recv, a_send, a_recv, s_send, s_recv,
):
    ctx = lax.axis_index("ctx")
    dec = lax.axis_index("dec")
    core = ctx % 2
    z = ctx // 4
    x = dec // 2
    y = (dec % 2) * 2 + (ctx // 2) % 2
    first = core == 0
    a = jnp.where(first, x, y)
    b = jnp.where(first, y, x)

    def at_ab(aa, bb):
        return device(jnp.where(first, aa, bb), jnp.where(first, bb, aa), z, core)

    half_me = (x // 2 + dec % 2) % 2
    sub_me = (x % 2) * 2 + dec % 2
    low_at = jnp.minimum(order_ref[ctx * 2], order_ref[ctx * 2 + 1]) * HALF
    high_at = jnp.maximum(order_ref[ctx * 2], order_ref[ctx * 2 + 1]) * HALF
    turn = jnp.full((HALF * HEADS, LAT), order_ref[ctx * 2], jnp.int32) > order_ref[ctx * 2 + 1]

    rs_offsets = [(2, 1), (1, 1), (3, 1), (2, 0), (0, 1), (1, 0), (3, 0)]

    def rs_device(dx, dy, sign):
        xx = (x + sign * dx + NX) % NX
        yh = (dec % 2 + dy) % 2
        return ctx, xx * 2 + yh

    loads = [pltpu.make_async_copy(hidden_hbm, hid, in_sem.at[0])]
    for k in range(4):
        span = pl.ds(k * 144, 144)
        loads.append(pltpu.make_async_copy(weight_hbm.at[span], wt.at[span], in_sem.at[1 + k]))
    for k in range(4):
        span = pl.ds(k * 2, 2)
        loads.append(pltpu.make_async_copy(queries_hbm.at[span], qt.at[span], in_sem.at[5 + k]))
    for load in loads:
        load.start()

    barrier = pltpu.get_barrier_semaphore()
    partners = [rs_device(dx, dy, 1) for dx, dy in rs_offsets]
    partners += [device(x, y, (z + dz) % NZ, core) for dz in range(1, NZ)]
    partners += [at_ab(a, (b + d) % 4) for d in range(1, 4)]
    partners += [at_ab((a + d) % 4, b) for d in range(1, 4)]
    partners += [device(x, y, z, 1 - core)]
    for target in partners:
        pl.semaphore_signal(barrier, inc=1, device_id=target, device_id_type=MESH)

    for load in loads[:5]:
        load.wait()
    projected = lax.dot_general(
        hid[...], wt[...], (((1,), (1,)), ((), ())), preferred_element_type=jnp.float32
    )
    upper, lower = projected[:HALF], projected[HALF:]
    swap = jnp.full(upper.shape, order_ref[ctx * 2], jnp.int32) > order_ref[ctx * 2 + 1]
    part[:4] = jnp.where(swap, lower, upper).reshape(4, PIECE, LAT + ROT)
    part[4:] = jnp.where(swap, upper, lower).reshape(4, PIECE, LAT + ROT)
    pl.semaphore_wait(barrier, len(partners))

    scatter = []
    for k, (dx, dy) in enumerate(rs_offsets):
        target = rs_device(dx, dy, 1)
        tx, ty = target[1] // 2, target[1] % 2
        theirs = ((tx // 2 + ty) % 2) * 4 + (tx % 2) * 2 + ty
        scatter.append(remote(part.at[theirs], sums.at[k], rs_send.at[k], rs_recv.at[k], target))
        scatter[-1].start()

    start_pos = jnp.where(half_me == 0, low_at, high_at) + sub_me * PIECE
    my_pos = (start_pos + lax.broadcasted_iota(jnp.int32, (PIECE, 128), 0)).astype(jnp.float32)
    angle = my_pos * freq_ref[...]
    cosine = jnp.cos(angle)
    sine = jnp.sin(angle)

    lane = lax.broadcasted_iota(jnp.int32, (1, ROWS), 1)
    lane_z = lane // PIECE
    lane_i = lane % PIECE
    mine = owner_ref[...] == ctx
    page_id = lax.broadcasted_iota(jnp.int32, (PAGES, PAGES), 1).astype(jnp.float32)
    page_of = jnp.sum(jnp.where(mine, page_id, 0.0), axis=1, keepdims=True)
    slot_of = jnp.sum(jnp.where(mine, slot_ref[...].astype(jnp.float32), 0.0), axis=1, keepdims=True)
    ctx_id = lax.broadcasted_iota(jnp.int32, (PAGES, ROWS), 0)
    place_lane = lax.broadcasted_iota(jnp.int32, (PAGES, ROWS), 1) // PIECE
    ctx_lane = jnp.zeros((PAGES, ROWS), jnp.int32)
    for at, step in enumerate(STEPS):
        ctx_lane = jnp.where(place_lane == at, (z + step) % NZ, ctx_lane)
    for cc in range(2):
        for ylo in range(2):
            picks = ctx_id == ctx_lane * 4 + (ylo * 2 + cc)
            page_z = jnp.sum(jnp.where(picks, page_of, 0.0), axis=0, keepdims=True).astype(jnp.int32)
            slot_z = jnp.sum(jnp.where(picks, slot_of, 0.0), axis=0, keepdims=True).astype(jnp.int32)
            bases = [jnp.zeros((1, ROWS), jnp.int32)] * 2
            turned = jnp.zeros((1, ROWS), jnp.int32)
            for zz, step in enumerate(STEPS):
                at = (((z + step) % NZ * 2 + ylo) * 2 + cc) * 2
                one, two = order_ref[at], order_ref[at + 1]
                bases[0] = jnp.where(lane_z == zz, jnp.minimum(one, two) * HALF, bases[0])
                bases[1] = jnp.where(lane_z == zz, jnp.maximum(one, two) * HALF, bases[1])
                turned = jnp.where(lane_z == zz, jnp.where(one > two, PAGES // 2, 0), turned)
            page_z = jnp.bitwise_xor(page_z, turned)
            for xx in range(4):
                for yhi in range(2):
                    aa, bb = (xx, yhi * 2 + ylo) if cc == 0 else (yhi * 2 + ylo, xx)
                    half, sub = (xx // 2 + yhi) % 2, (xx % 2) * 2 + yhi
                    row = (cc * 4 + aa) * 4 + bb
                    kpos[row : row + 1, :] = bases[half] + sub * PIECE + lane_i
                    page = half * (PAGES // 2) + sub * 4 + lane_i // 4
                    drow[row : row + 1, :] = jnp.where(page_z == page, (lane_i % 4) * PAGES + slot_z, -1)

    for load in loads[5:]:
        load.wait()
    rows = HEADS * ROWS
    for h in range(HEADS):
        turned = qt[h].T.astype(jnp.float32)
        turned = jnp.concatenate([turned, turned[:, LAT:]], axis=1)
        for g in range(5):
            q32[g, pl.ds(h, ROWS, stride=HEADS), :] = turned[:, g * 128 : (g + 1) * 128]
    for g in range(5):
        upper, lower = q32[g, : rows // 2, :], q32[g, rows // 2 :, :]
        swap = turn[:, :128]
        ordered = jnp.concatenate([jnp.where(swap, lower, upper), jnp.where(swap, upper, lower)], axis=0)
        if g < 4:
            ql[:, g * 128 : (g + 1) * 128] = ordered.astype(jnp.bfloat16)
        else:
            qr[...] = ordered.astype(jnp.bfloat16)
    qpos[...] = lax.broadcasted_iota(jnp.int32, qpos.shape, 0) // HEADS
    acc[...] = jnp.zeros_like(acc)
    den[...] = jnp.zeros_like(den)
    top[...] = jnp.full_like(top, NEG)
    page_lat[...] = jnp.zeros_like(page_lat)
    page_rot[...] = jnp.zeros_like(page_rot)

    total = part[half_me * 4 + sub_me]
    for k, copy in enumerate(scatter):
        copy.wait_recv()
        total = total + sums[k]

    latent = total[:, :LAT]
    inverse = lax.rsqrt(jnp.mean(latent * latent, axis=1, keepdims=True) + EPS)
    latent = latent * inverse * gain_ref[...]
    half = ROT // 2
    r1, r2 = total[:, LAT : LAT + half], total[:, LAT + half :]
    c1, s1 = cosine[:, :half], sine[:, :half]
    turned = jnp.concatenate([r1 * c1 - r2 * s1, r1 * s1 + r2 * c1], axis=1)
    zbuf[z] = jnp.concatenate([latent, turned, turned], axis=1).astype(jnp.bfloat16)

    along_z = []
    for dz in (7, 1, 6, 4, 3, 5, 2):
        copy = remote(zbuf.at[z], zbuf.at[z], z_send.at[dz], z_recv.at[dz], device(x, y, (z + dz) % NZ, core))
        copy.start()
        along_z.append(copy)
    left = lax.broadcasted_iota(jnp.int32, (PIECE, 128), 1) < ROT
    mine_block = gath.at[core, a, b]

    def settle(places):
        for at in places:
            came = (z + STEPS[at]) % NZ
            dz = (NZ - STEPS[at]) % NZ
            if dz > 0:
                remote(
                    zbuf.at[came], zbuf.at[came], z_send.at[dz], z_recv.at[dz], device(x, y, (z + dz) % NZ, core)
                ).wait_recv()
        for at in places:
            mine_block[at * PIECE : (at + 1) * PIECE, :] = zbuf[(z + STEPS[at]) % NZ, :, :LAT]

    sibling = device(x, y, z, 1 - core)

    def block(d, e):
        return gath.at[core, (a - d + 4) % 4, (b - e + 4) % 4]

    def some(ref, h):
        return ref.at[pl.ds(0, EARLY)] if h == 0 else ref.at[pl.ds(EARLY, BLOCK - EARLY)]

    def along_b(e, h):
        return remote(some(mine_block, h), some(mine_block, h), b_send.at[e, h], b_recv.at[e, h], at_ab(a, (b + e) % 4))

    def own_along_a(d, h):
        col = 4 * (1 - h)
        return remote(
            some(mine_block, h), some(mine_block, h), a_send.at[d, col], a_recv.at[d, col], at_ab((a + d) % 4, b)
        )

    def along_a(d, e):
        return remote(block(0, e), block(0, e), a_send.at[d, e], a_recv.at[d, e], at_ab((a + d) % 4, b))

    def across(d, e):
        return remote(block(d, e), block(d, e), s_send.at[d, e], s_recv.at[d, e], sibling)

    def onward(e):
        came, to = (block(1, e), a + 1) if e in (0, 1) else (block(3, e), a + 3)
        return remote(came, came, a_send.at[2, e], a_recv.at[2, e], at_ab(to % 4, b))

    def arrived(d, e):
        came = block(d, e)
        if e == 0 and d != 2:
            for h in range(2):
                col = 4 * (1 - h)
                remote(
                    some(came, h), some(came, h), a_send.at[d, col], a_recv.at[d, col], at_ab((a + d) % 4, b)
                ).wait_recv()
        else:
            remote(came, came, a_send.at[d, e], a_recv.at[d, e], at_ab((a + d) % 4, b)).wait_recv()

    def take(d, e):
        arrived(d, e)
        if (d, e) in ((1, 0), (1, 1), (3, 2), (3, 3)):
            onward(e).start()
        across(d, e).start()

    for h in range(2):
        settle(range(4 * h, 4 * h + 4))
        if h == 1:
            for pair in range(NZ // 2):
                mine_block[ROWS:, pair * 128 : (pair + 1) * 128] = jnp.where(
                    left,
                    zbuf[(z + STEPS[2 * pair]) % NZ, :, LAT:],
                    zbuf[(z + STEPS[2 * pair + 1]) % NZ, :, LAT:],
                )
        for e in (1, 3):
            along_b(e, h).start()
        for d in (1, 3):
            own_along_a(d, h).start()
    for e in (0, 1, 3, 2):
        if e > 0:
            for h in range(2):
                came = some(block(0, e), h)
                remote(came, came, b_send.at[e, h], b_recv.at[e, h], at_ab(a, (b + e) % 4)).wait_recv()
                if (e, h) in ((1, 0), (3, 1)):
                    remote(came, came, b_send.at[2, h], b_recv.at[2, h], at_ab(a, (b + e) % 4)).start()
            for d in (1, 3) if e == 1 else (3, 1):
                along_a(d, e).start()
        across(0, e).start()
        if e == 3:
            take(1, 0)
            take(3, 0)

    page_row = lax.broadcasted_iota(jnp.int32, (ROWS, CHUNK), 0)

    def attend(cc, pa, pb, k):
        near = jnp.logical_or(k == 1, k == 2)
        strip = (pa + jnp.where(k == 3, 2, 0)) % 4
        order = []
        for at in range(4):
            bb_near = (pb - 2 * (k - 1) - at % 2 + 8) % 4
            half = bb_near // 2 if at < 2 else 1 - bb_near // 2
            aa_near = half * 2 + (pa + 1) % 2
            bb_strip = (strip // 2 if at < 2 else 1 - strip // 2) * 2 + at % 2
            order.append((jnp.where(near, aa_near, strip), jnp.where(near, bb_near, bb_strip)))
        which = [(cc * 4 + aa) * 4 + bb for aa, bb in order]
        row_of = jnp.concatenate([drow[pl.ds(w, 1), :] for w in which], axis=1)
        pick = jnp.where(row_of == page_row, 1.0, 0.0).astype(jnp.bfloat16)
        for at, (aa, bb) in enumerate(order):
            for zz in range(NZ):
                rot = gath[cc, aa, bb, ROWS:, (zz // 2) * 128 : (zz // 2 + 1) * 128]
                keep = left if zz % 2 == 0 else jnp.logical_not(left)
                krot[at * ROWS + zz * PIECE : at * ROWS + (zz + 1) * PIECE, :] = jnp.where(
                    keep, rot, jnp.zeros_like(rot)
                )

        def keys(count=4):
            return jnp.concatenate([gath[cc, aa, bb, :ROWS, :] for aa, bb in order[:count]], axis=0)

        page_lat[...] += jnp.dot(pick, keys(), preferred_element_type=jnp.float32)
        page_rot[...] += jnp.dot(pick, krot[...], preferred_element_type=jnp.float32)

        nt = (((1,), (1,)), ((), ()))
        kp = jnp.concatenate([kpos[pl.ds(w, 1), :] for w in which], axis=1)
        near = CHUNK // 2

        def logits(rows, count):
            scores = lax.dot_general(ql[rows, :], keys(count), nt, preferred_element_type=jnp.float32)
            return scores + lax.dot_general(
                qr[rows, :], krot[: count * ROWS, :], nt, preferred_element_type=jnp.float32
            )

        def fold(rows, scores, count):
            old = top[rows, :]
            new = jnp.maximum(old, jnp.max(scores, axis=1, keepdims=True))
            alpha = jnp.exp2((old - new) * LOG2E_SCALE)
            weights = jnp.exp2((scores - jnp.concatenate([new] * count, axis=1)) * LOG2E_SCALE)
            top[rows, :] = new
            summed = weights[:, :128]
            for part_at in range(1, count):
                summed += weights[:, part_at * 128 : (part_at + 1) * 128]
            den[rows, :] = den[rows, :] * alpha + summed
            mixed = jnp.dot(weights.astype(jnp.bfloat16), keys(count), preferred_element_type=jnp.float32)
            acc[rows, :] = acc[rows, :] * jnp.concatenate([alpha] * 4, axis=1) + mixed

        low_rows, high_rows = slice(0, HALF * HEADS), slice(HALF * HEADS, 2 * HALF * HEADS)
        limit = jnp.concatenate([qpos[...]] * 2, axis=1)
        high = logits(high_rows, 4)
        low = logits(low_rows, 2)
        high = jnp.concatenate(
            [high[:, :near], jnp.where(kp[:, near:] - high_at <= limit, high[:, near:], NEG)], axis=1
        )
        low = jnp.where(kp[:, :near] - low_at <= limit, low, NEG)
        fold(high_rows, high, 4)
        fold(low_rows, low, 2)

    @pl.loop(0, 4)
    def _(k):
        @pl.when(k == 3)
        def _():
            for e in (3, 2):
                arrived(2, e)
                across(2, e).start()

        attend(core, a, b, k)

        @pl.when(k == 0)
        def _():
            for d, e in ((1, 1), (3, 3), (3, 1), (1, 3)):
                take(d, e)

        @pl.when(k == 1)
        def _():
            for d, e in ((3, 2), (1, 2)):
                take(d, e)

        @pl.when(k == 2)
        def _():
            for e in (0, 1):
                arrived(2, e)
                across(2, e).start()

        near = jnp.logical_or(k == 1, k == 2)
        for at in range(4):
            d = jnp.where(near, 1 + 2 * (at % 2), jnp.where(k == 3, 2, 0))
            e = jnp.where(near, jnp.where(k == 1, at // 2, 3 - at // 2), at)
            there = gath.at[1 - core, (b - d + 4) % 4, (a - e + 4) % 4]
            remote(there, there, s_send.at[d, e], s_recv.at[d, e], sibling).wait_recv()
        attend(1 - core, b, a, k)

    for k in range(4):
        low_span, high_span = slice(k * ROWS, (k + 1) * ROWS), slice((k + 4) * ROWS, (k + 5) * ROWS)
        low = acc[low_span, :] / jnp.sum(den[low_span, :], axis=1, keepdims=True)
        high = acc[high_span, :] / jnp.sum(den[high_span, :], axis=1, keepdims=True)
        swap = turn[:ROWS]
        out_ref[low_span, :] = jnp.where(swap, high, low).astype(jnp.bfloat16)
        out_ref[high_span, :] = jnp.where(swap, low, high).astype(jnp.bfloat16)

    rotated = page_rot[:, :ROT] + page_rot[:, ROT:]
    width = LAT + ROT
    for j in range(4):
        span = slice(j * PAGES, (j + 1) * PAGES)
        paged_ref[:, j * width : j * width + LAT] = page_lat[span, :].astype(jnp.bfloat16)
        paged_ref[:, j * width + LAT : (j + 1) * width] = rotated[span, :].astype(jnp.bfloat16)

    for copy in scatter + along_z:
        copy.wait_send()
    for e in range(4):
        if e > 0:
            for h in range(2):
                along_b(e, h).wait_send()
        for d in (1, 3):
            if e > 0:
                along_a(d, e).wait_send()
            else:
                own_along_a(d, 0).wait_send()
                own_along_a(d, 1).wait_send()
        onward(e).wait_send()
        for d in range(4):
            across(d, e).wait_send()


def body(hidden, kv_weight, kv_gain, queries, group_order, page_owner, page_slot):
    half = ROT // 2
    freq = 10000.0 ** (-(2.0 * np.arange(half, dtype=np.float32)) / ROT)
    freq = np.tile(freq.astype(np.float32), 4)[None, :]
    bf, f32 = jnp.bfloat16, jnp.float32
    vmem = pl.BlockSpec(memory_space=pltpu.VMEM)
    hbm = pl.BlockSpec(memory_space=pl.ANY)
    smem = pl.BlockSpec(memory_space=pltpu.SMEM)
    rows = HEADS * ROWS
    dma = pltpu.SemaphoreType.DMA
    attended, paged = pl.pallas_call(
        kernel,
        out_shape=(
            pltpu.VMEM((rows, LAT), bf),
            pltpu.VMEM((PAGES, 4 * (LAT + ROT)), bf),
        ),
        in_specs=[hbm, hbm, vmem, vmem, hbm, smem, vmem, vmem],
        out_specs=(vmem, vmem),
        scratch_shapes=[
            pltpu.VMEM(hidden.shape, bf),
            pltpu.VMEM(kv_weight.shape[::-1], bf),
            pltpu.VMEM((HEADS, LAT + ROT, ROWS), bf),
            pltpu.VMEM((8, PIECE, LAT + ROT), f32),
            pltpu.VMEM((7, PIECE, LAT + ROT), f32),
            pltpu.VMEM((NZ, PIECE, LAT + 128), bf),
            pltpu.VMEM((2, 4, 4, BLOCK, LAT), bf),
            pltpu.VMEM((5, rows, 128), f32),
            pltpu.VMEM((rows, LAT), bf),
            pltpu.VMEM((rows, 128), bf),
            pltpu.VMEM((rows, LAT), f32),
            pltpu.VMEM((rows, 128), f32),
            pltpu.VMEM((rows, 128), f32),
            pltpu.VMEM((rows // 2, 128), jnp.int32),
            pltpu.VMEM((32, ROWS), jnp.int32),
            pltpu.VMEM((32, ROWS), jnp.int32),
            pltpu.VMEM((ROWS, LAT), f32),
            pltpu.VMEM((ROWS, 128), f32),
            pltpu.VMEM((CHUNK, 128), bf),
            dma((9,)), dma((7,)), dma((7,)), dma((8,)), dma((8,)), dma((4, 2)), dma((4, 2)), dma((4, 5)), dma((4, 5)),
            dma((4, 4)), dma((4, 4)),
        ],
        name="cache_attention",
        compiler_params=pltpu.CompilerParams(
            collective_id=0, has_side_effects=True, vmem_limit_bytes=56 * 2**20
        ),
        cost_estimate=pl.CostEstimate(flops=9_000_000_000, bytes_accessed=4_000_000, transcendentals=4_000_000),
    )(
        hidden, kv_weight.T, kv_gain.reshape(1, -1), jnp.asarray(freq), queries.transpose(1, 2, 0),
        group_order, page_owner, page_slot,
    )
    return attended.reshape(ROWS, HEADS, LAT), paged


def solution(mesh):
    return jax.shard_map(
        body,
        mesh=mesh,
        in_specs=(P("ctx", "dec"), P("dec", None), P(), P("ctx", "dec", None), P(), P(), P()),
        out_specs=(P("ctx", "dec", None), P("ctx", None)),
        check_vma=False,
    )
```

```python
import functools

import jax
import jax.numpy as jnp
import numpy as np
from jax import lax
from jax.experimental import pallas as pl
from jax.experimental.pallas import tpu as pltpu
from jax.sharding import PartitionSpec as P

MESH = pl.DeviceIdType.MESH
NX, NY, NZ = 4, 4, 8
HALF = 64
ROWS = 128
PIECE = 16
LAT = 512
ROT = 64
HEADS = 8
BLOCK = ROWS + PIECE
CHUNK = 4 * ROWS
PAGES = 32
EPS = 1e-6
LOG2E_SCALE = float(192.0 ** (-0.5) * np.log2(np.e))
NEG = -1e30
STEPS = (0, 1, 7, 2, 6, 3, 5, 4)
EARLY = ROWS // 2


def device(x, y, z, core):
    return ((z * 2 + y % 2) * 2 + core, x * 2 + y // 2)


def remote(src, dst, send_sem, recv_sem, target):
    return pltpu.make_async_remote_copy(
        src_ref=src, dst_ref=dst, send_sem=send_sem, recv_sem=recv_sem, device_id=target, device_id_type=MESH
    )


def kernel(
    hidden_hbm, weight_hbm, gain_ref, freq_ref, queries_hbm, order_ref, owner_ref, slot_ref,
    out_ref, paged_ref,
    hid, wt, qt, part, sums, zbuf, gath, q32, ql, qr, acc, top, den, qpos, kpos, drow, page_lat, page_rot, krot,
    in_sem, rs_send, rs_recv, z_send, z_recv, b_send, b_recv, a_send, a_recv, s_send, s_recv,
):
    ctx = lax.axis_index("ctx")
    dec = lax.axis_index("dec")
    core = ctx % 2
    z = ctx // 4
    x = dec // 2
    y = (dec % 2) * 2 + (ctx // 2) % 2
    first = core == 0
    a = jnp.where(first, x, y)
    b = jnp.where(first, y, x)

    def at_ab(aa, bb):
        return device(jnp.where(first, aa, bb), jnp.where(first, bb, aa), z, core)

    half_me = (x // 2 + dec % 2) % 2
    sub_me = (x % 2) * 2 + dec % 2
    low_at = jnp.minimum(order_ref[ctx * 2], order_ref[ctx * 2 + 1]) * HALF
    high_at = jnp.maximum(order_ref[ctx * 2], order_ref[ctx * 2 + 1]) * HALF
    turn = jnp.full((HALF * HEADS, LAT), order_ref[ctx * 2], jnp.int32) > order_ref[ctx * 2 + 1]

    rs_offsets = [(2, 1), (1, 1), (3, 1), (2, 0), (0, 1), (1, 0), (3, 0)]

    def rs_device(dx, dy, sign):
        xx = (x + sign * dx + NX) % NX
        yh = (dec % 2 + dy) % 2
        return ctx, xx * 2 + yh

    loads = [pltpu.make_async_copy(hidden_hbm, hid, in_sem.at[0])]
    for k in range(4):
        span = pl.ds(k * 144, 144)
        loads.append(pltpu.make_async_copy(weight_hbm.at[span], wt.at[span], in_sem.at[1 + k]))
    for k in range(4):
        span = pl.ds(k * 2, 2)
        loads.append(pltpu.make_async_copy(queries_hbm.at[span], qt.at[span], in_sem.at[5 + k]))
    for load in loads:
        load.start()

    barrier = pltpu.get_barrier_semaphore()
    partners = [rs_device(dx, dy, 1) for dx, dy in rs_offsets]
    partners += [device(x, y, (z + dz) % NZ, core) for dz in range(1, NZ)]
    partners += [at_ab(a, (b + d) % 4) for d in range(1, 4)]
    partners += [at_ab((a + d) % 4, b) for d in range(1, 4)]
    partners += [device(x, y, z, 1 - core)]
    for target in partners:
        pl.semaphore_signal(barrier, inc=1, device_id=target, device_id_type=MESH)

    for load in loads[:5]:
        load.wait()
    projected = lax.dot_general(
        hid[...], wt[...], (((1,), (1,)), ((), ())), preferred_element_type=jnp.float32
    )
    upper, lower = projected[:HALF], projected[HALF:]
    swap = jnp.full(upper.shape, order_ref[ctx * 2], jnp.int32) > order_ref[ctx * 2 + 1]
    part[:4] = jnp.where(swap, lower, upper).reshape(4, PIECE, LAT + ROT)
    part[4:] = jnp.where(swap, upper, lower).reshape(4, PIECE, LAT + ROT)
    pl.semaphore_wait(barrier, len(partners))

    scatter = []
    for k, (dx, dy) in enumerate(rs_offsets):
        target = rs_device(dx, dy, 1)
        tx, ty = target[1] // 2, target[1] % 2
        theirs = ((tx // 2 + ty) % 2) * 4 + (tx % 2) * 2 + ty
        scatter.append(remote(part.at[theirs], sums.at[k], rs_send.at[k], rs_recv.at[k], target))
        scatter[-1].start()

    start_pos = jnp.where(half_me == 0, low_at, high_at) + sub_me * PIECE
    my_pos = (start_pos + lax.broadcasted_iota(jnp.int32, (PIECE, 128), 0)).astype(jnp.float32)
    angle = my_pos * freq_ref[...]
    cosine = jnp.cos(angle)
    sine = jnp.sin(angle)

    lane = lax.broadcasted_iota(jnp.int32, (1, ROWS), 1)
    lane_z = lane // PIECE
    lane_i = lane % PIECE
    mine = owner_ref[...] == ctx
    page_id = lax.broadcasted_iota(jnp.int32, (PAGES, PAGES), 1).astype(jnp.float32)
    page_of = jnp.sum(jnp.where(mine, page_id, 0.0), axis=1, keepdims=True)
    slot_of = jnp.sum(jnp.where(mine, slot_ref[...].astype(jnp.float32), 0.0), axis=1, keepdims=True)
    ctx_id = lax.broadcasted_iota(jnp.int32, (PAGES, ROWS), 0)
    place_lane = lax.broadcasted_iota(jnp.int32, (PAGES, ROWS), 1) // PIECE
    ctx_lane = jnp.zeros((PAGES, ROWS), jnp.int32)
    for at, step in enumerate(STEPS):
        ctx_lane = jnp.where(place_lane == at, (z + step) % NZ, ctx_lane)
    for cc in range(2):
        for ylo in range(2):
            picks = ctx_id == ctx_lane * 4 + (ylo * 2 + cc)
            page_z = jnp.sum(jnp.where(picks, page_of, 0.0), axis=0, keepdims=True).astype(jnp.int32)
            slot_z = jnp.sum(jnp.where(picks, slot_of, 0.0), axis=0, keepdims=True).astype(jnp.int32)
            bases = [jnp.zeros((1, ROWS), jnp.int32)] * 2
            turned = jnp.zeros((1, ROWS), jnp.int32)
            for zz, step in enumerate(STEPS):
                at = (((z + step) % NZ * 2 + ylo) * 2 + cc) * 2
                one, two = order_ref[at], order_ref[at + 1]
                bases[0] = jnp.where(lane_z == zz, jnp.minimum(one, two) * HALF, bases[0])
                bases[1] = jnp.where(lane_z == zz, jnp.maximum(one, two) * HALF, bases[1])
                turned = jnp.where(lane_z == zz, jnp.where(one > two, PAGES // 2, 0), turned)
            page_z = jnp.bitwise_xor(page_z, turned)
            for xx in range(4):
                for yhi in range(2):
                    aa, bb = (xx, yhi * 2 + ylo) if cc == 0 else (yhi * 2 + ylo, xx)
                    half, sub = (xx // 2 + yhi) % 2, (xx % 2) * 2 + yhi
                    row = (cc * 4 + aa) * 4 + bb
                    kpos[row : row + 1, :] = bases[half] + sub * PIECE + lane_i
                    page = half * (PAGES // 2) + sub * 4 + lane_i // 4
                    drow[row : row + 1, :] = jnp.where(page_z == page, (lane_i % 4) * PAGES + slot_z, -1)

    for load in loads[5:]:
        load.wait()
    rows = HEADS * ROWS
    for h in range(HEADS):
        turned = qt[h].T.astype(jnp.float32)
        turned = jnp.concatenate([turned, turned[:, LAT:]], axis=1)
        for g in range(5):
            q32[g, pl.ds(h, ROWS, stride=HEADS), :] = turned[:, g * 128 : (g + 1) * 128]
    for g in range(5):
        upper, lower = q32[g, : rows // 2, :], q32[g, rows // 2 :, :]
        swap = turn[:, :128]
        ordered = jnp.concatenate([jnp.where(swap, lower, upper), jnp.where(swap, upper, lower)], axis=0)
        if g < 4:
            ql[:, g * 128 : (g + 1) * 128] = ordered.astype(jnp.bfloat16)
        else:
            qr[...] = ordered.astype(jnp.bfloat16)
    qpos[...] = lax.broadcasted_iota(jnp.int32, qpos.shape, 0) // HEADS
    acc[...] = jnp.zeros_like(acc)
    den[...] = jnp.zeros_like(den)
    top[...] = jnp.full_like(top, NEG)
    page_lat[...] = jnp.zeros_like(page_lat)
    page_rot[...] = jnp.zeros_like(page_rot)

    total = part[half_me * 4 + sub_me]
    for k, copy in enumerate(scatter):
        copy.wait_recv()
        total = total + sums[k]

    latent = total[:, :LAT]
    inverse = lax.rsqrt(jnp.mean(latent * latent, axis=1, keepdims=True) + EPS)
    latent = latent * inverse * gain_ref[...]
    half = ROT // 2
    r1, r2 = total[:, LAT : LAT + half], total[:, LAT + half :]
    c1, s1 = cosine[:, :half], sine[:, :half]
    turned = jnp.concatenate([r1 * c1 - r2 * s1, r1 * s1 + r2 * c1], axis=1)
    zbuf[z] = jnp.concatenate([latent, turned, turned], axis=1).astype(jnp.bfloat16)

    along_z = []
    for dz in (7, 1, 6, 4, 3, 5, 2):
        copy = remote(zbuf.at[z], zbuf.at[z], z_send.at[dz], z_recv.at[dz], device(x, y, (z + dz) % NZ, core))
        copy.start()
        along_z.append(copy)
    left = lax.broadcasted_iota(jnp.int32, (PIECE, 128), 1) < ROT
    mine_block = gath.at[core, a, b]

    def settle(places):
        for at in places:
            came = (z + STEPS[at]) % NZ
            dz = (NZ - STEPS[at]) % NZ
            if dz > 0:
                remote(
                    zbuf.at[came], zbuf.at[came], z_send.at[dz], z_recv.at[dz], device(x, y, (z + dz) % NZ, core)
                ).wait_recv()
        for at in places:
            mine_block[at * PIECE : (at + 1) * PIECE, :] = zbuf[(z + STEPS[at]) % NZ, :, :LAT]

    sibling = device(x, y, z, 1 - core)

    def block(d, e):
        return gath.at[core, (a - d + 4) % 4, (b - e + 4) % 4]

    def some(ref, h):
        return ref.at[pl.ds(0, EARLY)] if h == 0 else ref.at[pl.ds(EARLY, BLOCK - EARLY)]

    def along_b(e, h):
        return remote(some(mine_block, h), some(mine_block, h), b_send.at[e, h], b_recv.at[e, h], at_ab(a, (b + e) % 4))

    def own_along_a(d, h):
        col = 4 * (1 - h)
        return remote(
            some(mine_block, h), some(mine_block, h), a_send.at[d, col], a_recv.at[d, col], at_ab((a + d) % 4, b)
        )

    def along_a(d, e):
        return remote(block(0, e), block(0, e), a_send.at[d, e], a_recv.at[d, e], at_ab((a + d) % 4, b))

    def across(d, e):
        return remote(block(d, e), block(d, e), s_send.at[d, e], s_recv.at[d, e], sibling)

    def onward(e):
        came, to = (block(1, e), a + 1) if e in (0, 1) else (block(3, e), a + 3)
        return remote(came, came, a_send.at[2, e], a_recv.at[2, e], at_ab(to % 4, b))

    def arrived(d, e):
        came = block(d, e)
        if e == 0 and d != 2:
            for h in range(2):
                col = 4 * (1 - h)
                remote(
                    some(came, h), some(came, h), a_send.at[d, col], a_recv.at[d, col], at_ab((a + d) % 4, b)
                ).wait_recv()
        else:
            remote(came, came, a_send.at[d, e], a_recv.at[d, e], at_ab((a + d) % 4, b)).wait_recv()

    def take(d, e):
        arrived(d, e)
        if (d, e) in ((1, 0), (1, 1), (3, 2), (3, 3)):
            onward(e).start()
        across(d, e).start()

    for h in range(2):
        settle(range(4 * h, 4 * h + 4))
        if h == 1:
            for pair in range(NZ // 2):
                mine_block[ROWS:, pair * 128 : (pair + 1) * 128] = jnp.where(
                    left,
                    zbuf[(z + STEPS[2 * pair]) % NZ, :, LAT:],
                    zbuf[(z + STEPS[2 * pair + 1]) % NZ, :, LAT:],
                )
        for e in (1, 3):
            along_b(e, h).start()
        for d in (1, 3):
            own_along_a(d, h).start()
    for e in (0, 1, 3, 2):
        if e > 0:
            for h in range(2):
                came = some(block(0, e), h)
                remote(came, came, b_send.at[e, h], b_recv.at[e, h], at_ab(a, (b + e) % 4)).wait_recv()
                if (e, h) in ((1, 0), (3, 1)):
                    remote(came, came, b_send.at[2, h], b_recv.at[2, h], at_ab(a, (b + e) % 4)).start()
            for d in (1, 3) if e == 1 else (3, 1):
                along_a(d, e).start()
        across(0, e).start()
        if e == 3:
            take(1, 0)
            take(3, 0)

    page_row = lax.broadcasted_iota(jnp.int32, (ROWS, CHUNK), 0)

    def attend(cc, pa, pb, k):
        near = jnp.logical_or(k == 1, k == 2)
        strip = (pa + jnp.where(k == 3, 2, 0)) % 4
        order = []
        for at in range(4):
            bb_near = (pb - 2 * (k - 1) - at % 2 + 8) % 4
            half = bb_near // 2 if at < 2 else 1 - bb_near // 2
            aa_near = half * 2 + (pa + 1) % 2
            bb_strip = (strip // 2 if at < 2 else 1 - strip // 2) * 2 + at % 2
            order.append((jnp.where(near, aa_near, strip), jnp.where(near, bb_near, bb_strip)))
        which = [(cc * 4 + aa) * 4 + bb for aa, bb in order]
        row_of = jnp.concatenate([drow[pl.ds(w, 1), :] for w in which], axis=1)
        pick = jnp.where(row_of == page_row, 1.0, 0.0).astype(jnp.bfloat16)
        for at, (aa, bb) in enumerate(order):
            for zz in range(NZ):
                rot = gath[cc, aa, bb, ROWS:, (zz // 2) * 128 : (zz // 2 + 1) * 128]
                keep = left if zz % 2 == 0 else jnp.logical_not(left)
                krot[at * ROWS + zz * PIECE : at * ROWS + (zz + 1) * PIECE, :] = jnp.where(
                    keep, rot, jnp.zeros_like(rot)
                )

        def keys(count=4):
            return jnp.concatenate([gath[cc, aa, bb, :ROWS, :] for aa, bb in order[:count]], axis=0)

        page_lat[...] += jnp.dot(pick, keys(), preferred_element_type=jnp.float32)
        page_rot[...] += jnp.dot(pick, krot[...], preferred_element_type=jnp.float32)

        nt = (((1,), (1,)), ((), ()))
        kp = jnp.concatenate([kpos[pl.ds(w, 1), :] for w in which], axis=1)
        near = CHUNK // 2

        def logits(rows, count):
            scores = lax.dot_general(ql[rows, :], keys(count), nt, preferred_element_type=jnp.float32)
            return scores + lax.dot_general(
                qr[rows, :], krot[: count * ROWS, :], nt, preferred_element_type=jnp.float32
            )

        def fold(rows, scores, count):
            old = top[rows, :]
            new = jnp.maximum(old, jnp.max(scores, axis=1, keepdims=True))
            alpha = jnp.exp2((old - new) * LOG2E_SCALE)
            weights = jnp.exp2((scores - jnp.concatenate([new] * count, axis=1)) * LOG2E_SCALE)
            top[rows, :] = new
            summed = weights[:, :128]
            for part_at in range(1, count):
                summed += weights[:, part_at * 128 : (part_at + 1) * 128]
            den[rows, :] = den[rows, :] * alpha + summed
            mixed = jnp.dot(weights.astype(jnp.bfloat16), keys(count), preferred_element_type=jnp.float32)
            acc[rows, :] = acc[rows, :] * jnp.concatenate([alpha] * 4, axis=1) + mixed

        low_rows, high_rows = slice(0, HALF * HEADS), slice(HALF * HEADS, 2 * HALF * HEADS)
        limit = jnp.concatenate([qpos[...]] * 2, axis=1)
        high = logits(high_rows, 4)
        low = logits(low_rows, 2)
        high = jnp.concatenate(
            [high[:, :near], jnp.where(kp[:, near:] - high_at <= limit, high[:, near:], NEG)], axis=1
        )
        low = jnp.where(kp[:, :near] - low_at <= limit, low, NEG)
        fold(high_rows, high, 4)
        fold(low_rows, low, 2)

    for copy in scatter + along_z:
        copy.wait_send()

    @pl.loop(0, 4)
    def _(k):
        @pl.when(k == 3)
        def _():
            for e in (3, 2):
                arrived(2, e)
                across(2, e).start()

        attend(core, a, b, k)

        @pl.when(k == 0)
        def _():
            for d, e in ((1, 1), (3, 3), (3, 1), (1, 3)):
                take(d, e)

        @pl.when(k == 1)
        def _():
            for d, e in ((3, 2), (1, 2)):
                take(d, e)

        @pl.when(k == 2)
        def _():
            for e in (0, 1):
                arrived(2, e)
                across(2, e).start()

        near = jnp.logical_or(k == 1, k == 2)
        for at in range(4):
            d = jnp.where(near, 1 + 2 * (at % 2), jnp.where(k == 3, 2, 0))
            e = jnp.where(near, jnp.where(k == 1, at // 2, 3 - at // 2), at)
            there = gath.at[1 - core, (b - d + 4) % 4, (a - e + 4) % 4]
            remote(there, there, s_send.at[d, e], s_recv.at[d, e], sibling).wait_recv()
        attend(1 - core, b, a, k)

    for k in range(4):
        low_span, high_span = slice(k * ROWS, (k + 1) * ROWS), slice((k + 4) * ROWS, (k + 5) * ROWS)
        low = acc[low_span, :] * (1.0 / jnp.sum(den[low_span, :], axis=1, keepdims=True))
        high = acc[high_span, :] * (1.0 / jnp.sum(den[high_span, :], axis=1, keepdims=True))
        swap = turn[:ROWS]
        out_ref[low_span, :] = jnp.where(swap, high, low).astype(jnp.bfloat16)
        out_ref[high_span, :] = jnp.where(swap, low, high).astype(jnp.bfloat16)

    rotated = page_rot[:, :ROT] + page_rot[:, ROT:]
    width = LAT + ROT
    for j in range(4):
        span = slice(j * PAGES, (j + 1) * PAGES)
        paged_ref[:, j * width : j * width + LAT] = page_lat[span, :].astype(jnp.bfloat16)
        paged_ref[:, j * width + LAT : (j + 1) * width] = rotated[span, :].astype(jnp.bfloat16)

    for e in range(4):
        if e > 0:
            for h in range(2):
                along_b(e, h).wait_send()
        for d in (1, 3):
            if e > 0:
                along_a(d, e).wait_send()
            else:
                own_along_a(d, 0).wait_send()
                own_along_a(d, 1).wait_send()
        onward(e).wait_send()
        for d in range(4):
            across(d, e).wait_send()


def body(hidden, kv_weight, kv_gain, queries, group_order, page_owner, page_slot):
    half = ROT // 2
    freq = 10000.0 ** (-(2.0 * np.arange(half, dtype=np.float32)) / ROT)
    freq = np.tile(freq.astype(np.float32), 4)[None, :]
    bf, f32 = jnp.bfloat16, jnp.float32
    vmem = pl.BlockSpec(memory_space=pltpu.VMEM)
    hbm = pl.BlockSpec(memory_space=pl.ANY)
    smem = pl.BlockSpec(memory_space=pltpu.SMEM)
    rows = HEADS * ROWS
    dma = pltpu.SemaphoreType.DMA
    attended, paged = pl.pallas_call(
        kernel,
        out_shape=(
            pltpu.VMEM((rows, LAT), bf),
            pltpu.VMEM((PAGES, 4 * (LAT + ROT)), bf),
        ),
        in_specs=[hbm, hbm, vmem, vmem, hbm, smem, vmem, vmem],
        out_specs=(vmem, vmem),
        scratch_shapes=[
            pltpu.VMEM(hidden.shape, bf),
            pltpu.VMEM(kv_weight.shape[::-1], bf),
            pltpu.VMEM((HEADS, LAT + ROT, ROWS), bf),
            pltpu.VMEM((8, PIECE, LAT + ROT), f32),
            pltpu.VMEM((7, PIECE, LAT + ROT), f32),
            pltpu.VMEM((NZ, PIECE, LAT + 128), bf),
            pltpu.VMEM((2, 4, 4, BLOCK, LAT), bf),
            pltpu.VMEM((5, rows, 128), f32),
            pltpu.VMEM((rows, LAT), bf),
            pltpu.VMEM((rows, 128), bf),
            pltpu.VMEM((rows, LAT), f32),
            pltpu.VMEM((rows, 128), f32),
            pltpu.VMEM((rows, 128), f32),
            pltpu.VMEM((rows // 2, 128), jnp.int32),
            pltpu.VMEM((32, ROWS), jnp.int32),
            pltpu.VMEM((32, ROWS), jnp.int32),
            pltpu.VMEM((ROWS, LAT), f32),
            pltpu.VMEM((ROWS, 128), f32),
            pltpu.VMEM((CHUNK, 128), bf),
            dma((9,)), dma((7,)), dma((7,)), dma((8,)), dma((8,)), dma((4, 2)), dma((4, 2)), dma((4, 5)), dma((4, 5)),
            dma((4, 4)), dma((4, 4)),
        ],
        name="cache_attention",
        compiler_params=pltpu.CompilerParams(
            collective_id=0, has_side_effects=True, vmem_limit_bytes=56 * 2**20
        ),
        cost_estimate=pl.CostEstimate(flops=9_000_000_000, bytes_accessed=4_000_000, transcendentals=4_000_000),
    )(
        hidden, kv_weight.T, kv_gain.reshape(1, -1), jnp.asarray(freq), queries.transpose(1, 2, 0),
        group_order, page_owner, page_slot,
    )
    return attended.reshape(ROWS, HEADS, LAT), paged


def solution(mesh):
    return jax.shard_map(
        body,
        mesh=mesh,
        in_specs=(P("ctx", "dec"), P("dec", None), P(), P("ctx", "dec", None), P(), P(), P()),
        out_specs=(P("ctx", "dec", None), P("ctx", None)),
        check_vma=False,
    )
```
